32 devices in a mesh: lat: 4 (over y, x), lon: 8 (over z, core).
Axes of the slice: x: 2, y: 2, z: 4, core: 2. Of those that a mesh axis runs over, the one named last changes fastest.
Arguments:
- tracer: float32 [6, 16, 32, 1024], P(None, None, 'lat', 'lon'), may hold values from -6 to 6
- east_vel: float32 [16, 32, 1024], P(None, 'lat', 'lon'), may hold values from -0.25 to 0.25
- north_vel: float32 [16, 32, 1024], P(None, 'lat', 'lon'), may hold values from -0.25 to 0.25
- wet_mask: int32 [16, 32, 1024], P(None, 'lat', 'lon'), may hold values from 0 to 1, as said below
- bottom_level: int32 [32, 1024], P('lat', 'lon'), may hold values from 0 to 16, as said below
- vertical_mix: float32 [16, 32, 1024], P(None, 'lat', 'lon'), may hold values from 0.05 to 5
Outputs:
- updated: float32 [6, 16, 32, 1024], P(None, None, 'lat', 'lon')
The draws below stay inside these ranges and needn't reach their ends.
Inputs may be any that keep to these rules, and one draw needn't show every extreme that they name: bottom_level is the number of levels above a column's sea floor; 0 on land. wet_mask is 0 at every level at or below its column's bottom_level.
All inputs are finite; a program needn't handle non-finite values.
Results may differ from the reference program's by a relative error of at most 0.00002.
Values sent between devices are 32-bit elements; how exact they have to be, the bound alone decides.
A program may use at most 64 MiB of HBM per device.

```python
import math
import jax
import jax.numpy as jnp
from jax import lax

NT = 6
K = 16
NY = 32
NX = 1024


def land_columns(key):
    coarse_rows = (NY + 15) // 16
    coarse_cols = (NX + 15) // 16
    blocks = jax.random.randint(jax.random.fold_in(key, 11), (coarse_rows, coarse_cols), 0, 4)
    row_ids = lax.broadcasted_iota(jnp.int32, (NY, NX), 0)
    col_ids = lax.broadcasted_iota(jnp.int32, (NY, NX), 1)
    inner_rows = (row_ids % 4 == 1) | (row_ids % 4 == 2)
    inner_cols = (col_ids % 4 == 1) | (col_ids % 4 == 2)
    land_cells = jnp.repeat(jnp.repeat(blocks == 0, 16, axis=0), 16, axis=1)[:NY, :NX] & inner_rows & inner_cols
    depths = jax.random.randint(jax.random.fold_in(key, 12), (NY, NX), 1, K + 1)
    marker = (col_ids + 3 * row_ids) % 37
    depths = jnp.where(land_cells, 0, depths)
    depths = jnp.where(marker == 0, K, depths)
    depths = jnp.where(marker == 1, 0, depths)
    return depths.astype(jnp.int32)


def draw_bottom_level(key, part):
    columns = land_columns(key)
    return columns


def draw_wet_mask(key, part):
    columns = land_columns(key)
    key = jax.random.fold_in(key, 5)
    sprinkle = jax.random.randint(key, (K, NY, NX), 0, 8) != 0
    level_ids = lax.broadcasted_iota(jnp.int32, (K, NY, NX), 0)
    return ((level_ids < columns[None, :, :]) & sprinkle).astype(jnp.int32)


def block_levels(key, extent, shards, least, top_value):
    loudness = 1.0
    for axis_at, parts in shards:
        steps = jax.random.uniform(jax.random.fold_in(jax.random.fold_in(key, 6), axis_at), (parts,), jnp.float32, least / len(shards), top_value / len(shards))
        loudness = loudness * jnp.repeat(jnp.exp(steps), extent[axis_at] // parts).reshape((-1,) + (1,) * (len(extent) - 1 - axis_at))
    return loudness


def scatter_about(key, extent, spread, reach, cuts=(), kind=jnp.bfloat16):
    gain = block_levels(key, extent, cuts, -0.22, 0.18) if cuts else 1.0
    values = jax.random.normal(key, extent, jnp.float32) * spread * gain
    return jnp.minimum(jnp.maximum(values, -reach), reach).astype(kind)


def setup_inputs(seed: int = 0) -> dict:
    keys = jax.random.split(jax.random.key(seed), 7)
    return {
        "tracer": scatter_about(keys[0], (NT, K, NY, NX), 1.0, 6.0, ((2, 4), (3, 8)), jnp.float32),
        "east_vel": jnp.clip(jax.random.uniform(keys[1], (K, NY, NX), jnp.float32, -0.25, 0.25) * block_levels(keys[1], (K, NY, NX), ((1, 4), (2, 8)), -0.4, 0.0), -0.25, 0.25),
        "north_vel": jnp.clip(jax.random.uniform(keys[2], (K, NY, NX), jnp.float32, -0.25, 0.25) * block_levels(keys[2], (K, NY, NX), ((1, 4), (2, 8)), -0.4, 0.0), -0.25, 0.25),
        "wet_mask": draw_wet_mask(jax.random.fold_in(keys[6], 71), 0),
        "bottom_level": draw_bottom_level(jax.random.fold_in(keys[6], 71), 0),
        "vertical_mix": jnp.clip(jnp.exp(math.log(5.0) - 4.6051702 * jax.random.uniform(keys[5], (K, NY, NX), jnp.float32) ** block_levels(keys[5], (K, NY, NX), ((1, 4), (2, 8)), -0.2, 0.2)), 0.05, 5.0),
    }


lateral_mixing = 0.08


def pad_global(field, sign_value):
    wrapped = jnp.concatenate([field[..., -1:], field, field[..., :1]], axis=-1)
    north_rows = sign_value * wrapped[..., -1:, ::-1]
    south_rows = jnp.zeros_like(north_rows)
    return jnp.concatenate([south_rows, wrapped, north_rows], axis=-2)


def flux_sum(tracer_pad, east_pad, north_pad, mask_pad):
    east_speed = 0.5 * (east_pad[..., 1:-1, :-1] + east_pad[..., 1:-1, 1:])
    east_open = mask_pad[..., 1:-1, :-1] * mask_pad[..., 1:-1, 1:]
    west_side = tracer_pad[..., 1:-1, :-1]
    east_side = tracer_pad[..., 1:-1, 1:]
    east_flux = east_open * (jnp.maximum(east_speed, 0.0) * west_side + jnp.minimum(east_speed, 0.0) * east_side - lateral_mixing * (east_side - west_side))
    north_speed = 0.5 * (north_pad[..., :-1, 1:-1] + north_pad[..., 1:, 1:-1])
    north_open = mask_pad[..., :-1, 1:-1] * mask_pad[..., 1:, 1:-1]
    south_side = tracer_pad[..., :-1, 1:-1]
    north_side = tracer_pad[..., 1:, 1:-1]
    north_flux = north_open * (jnp.maximum(north_speed, 0.0) * south_side + jnp.minimum(north_speed, 0.0) * north_side - lateral_mixing * (north_side - south_side))
    return mask_pad[..., 1:-1, 1:-1] * (((east_flux[..., :-1] - east_flux[..., 1:]) + north_flux[..., :-1, :]) - north_flux[..., 1:, :])


def solve_columns(rhs_field, couple):
    level_count = couple.shape[0]
    ratios = []
    values = []
    upper_c = couple[0]
    denom = 1.0 + upper_c
    ratio_prev = -upper_c / denom
    value_prev = rhs_field[..., 0, :, :] / denom
    ratios.append(ratio_prev)
    values.append(value_prev)
    for level_index in range(1, level_count):
        lower_c = couple[level_index - 1]
        upper_c = couple[level_index]
        denom = 1.0 + lower_c + upper_c + lower_c * ratio_prev
        ratio_prev = -upper_c / denom
        value_prev = (rhs_field[..., level_index, :, :] + lower_c * value_prev) / denom
        ratios.append(ratio_prev)
        values.append(value_prev)
    result_rows = [values[level_count - 1]]
    for level_index in range(level_count - 2, -1, -1):
        result_rows.append(values[level_index] - ratios[level_index] * result_rows[-1])
    return jnp.stack(result_rows[::-1], axis=-3)


def reference(tracer, east_vel, north_vel, wet_mask, bottom_level, vertical_mix):
    mask_float = wet_mask.astype(jnp.float32)
    east_pad = pad_global(east_vel, -1.0)
    north_pad = pad_global(north_vel, -1.0)
    mask_pad = pad_global(mask_float, 1.0)
    level_ids = lax.broadcasted_iota(jnp.int32, vertical_mix.shape, 0)
    couple = jnp.where(level_ids + 1 < bottom_level[None, :, :], vertical_mix, jnp.float32(0.0))

    def one_tracer(field_now):
        section_one = field_now + flux_sum(pad_global(field_now, 1.0), east_pad, north_pad, mask_pad)
        section_two = 0.5 * ((field_now + section_one) + flux_sum(pad_global(section_one, 1.0), east_pad, north_pad, mask_pad))
        return solve_columns(section_two, couple)

    return lax.map(one_tracer, tracer)
```

```python
import functools

import jax
import jax.numpy as jnp
from jax import lax
from jax.experimental import pallas as pl
from jax.experimental.pallas import tpu as pltpu
from jax.sharding import PartitionSpec as P

lateral_mixing = 0.08
MESH = pl.DeviceIdType.MESH
HIGH = lax.Precision.HIGHEST
ROWS, COLS = 8, 128
UNROLL = 2


def over_levels(count, body, carry, backward=False):
    def some(step, carry):
        for part in range(UNROLL):
            level = step * UNROLL + part
            if backward:
                level = count - 1 - level
            carry = body(level, carry)
        return carry

    return lax.fori_loop(0, count // UNROLL, some, carry)


def kernel(
    nt, k, n_lat, n_lon,
    t_hbm, u_hbm, v_hbm, m_hbm, b_hbm, mix_hbm, out,
    t, u, v, mi, b, mix, m, s1, rhs, y, coef, edge, solve,
    ns_send, ns_recv, ew_send, ew_recv, ns_send2, ns_recv2, ew_send2, ew_recv2,
    load_sem, send_sem, recv_sem,
):
    lat, lon = lax.axis_index("lat"), lax.axis_index("lon")
    is_top = lat == n_lat - 1
    has_south = lat > 0
    east = lax.rem(lon + 1, n_lon)
    west = lax.rem(lon + n_lon - 1, n_lon)
    north_id = (jnp.where(is_top, lat, lat + 1), jnp.where(is_top, n_lon - 1 - lon, lon))
    south_id = (jnp.where(has_south, lat - 1, lat), lon)
    top_flag = jnp.where(is_top, 1, 0)
    cells = k * ROWS

    loads = [
        pltpu.make_async_copy(src, dst, load_sem.at[i])
        for i, (src, dst) in enumerate(
            ((t_hbm, t), (v_hbm, v), (m_hbm, mi), (u_hbm, u), (b_hbm, b), (mix_hbm, mix))
        )
    ]
    for load in loads:
        load.start()

    barrier = pltpu.get_barrier_semaphore()
    for target in ((lat, east), (lat, west), north_id):
        pl.semaphore_signal(barrier, inc=1, device_id=target, device_id_type=MESH)

    @pl.when(has_south)
    def _():
        pl.semaphore_signal(barrier, inc=1, device_id=south_id, device_id_type=MESH)

    @pl.when(jnp.logical_not(has_south))
    def _():
        ns_recv[0] = jnp.zeros_like(ns_recv[0])
        ns_recv2[0] = jnp.zeros_like(ns_recv2[0])

    lane = lax.broadcasted_iota(jnp.int32, (ROWS, COLS), 1)
    row = lax.broadcasted_iota(jnp.int32, (ROWS, COLS), 0)
    pick_row = lax.broadcasted_iota(jnp.int32, (16, COLS), 0)
    pick_lane = lax.broadcasted_iota(jnp.int32, (16, COLS), 1)

    def picker(f):
        chosen = ((pick_row == f) & (pick_lane == 0)) | ((pick_row == 8 + f) & (pick_lane == COLS - 1))
        return jnp.where(chosen, 1.0, 0.0).astype(jnp.float32)

    def pack_rows(fields, send, flip_at):
        for side, at in ((0, 0), (1, ROWS - 1)):
            for f, (ref, base) in enumerate(fields):
                send[side, pl.ds(f * k, k), :] = ref[pl.ds(base + at, k, stride=ROWS), :]

        @pl.when(is_top)
        def _():
            a = lax.broadcasted_iota(jnp.int32, (COLS, COLS), 0)
            c = lax.broadcasted_iota(jnp.int32, (COLS, COLS), 1)
            mirror = jnp.where(a + c == COLS - 1, 1.0, 0.0).astype(jnp.float32)
            turned = jnp.dot(send[1], mirror, precision=HIGH, preferred_element_type=jnp.float32)
            if flip_at is not None:
                at_row = lax.broadcasted_iota(jnp.int32, turned.shape, 0)
                flips = (at_row >= flip_at) & (at_row < flip_at + k)
                turned = jnp.where(flips, -turned, turned)
            send[1] = turned

    def pack_columns(fields, send):
        total = jnp.zeros((16, COLS), jnp.float32)
        for f, (ref, base) in enumerate(fields):
            total += lax.dot_general(
                picker(f), ref[pl.ds(base, cells), :], (((1,), (1,)), ((), ())),
                precision=HIGH, preferred_element_type=jnp.float32,
            )
        send[...] = total

    def unpack_columns(count, recv):
        turned = recv[...].T
        for f in range(count):
            y[pl.ds(f * cells, cells), :] = jnp.dot(
                turned, picker(f), precision=HIGH, preferred_element_type=jnp.float32
            )

    def remote(src, dst, phase, way, land, target):
        return pltpu.make_async_remote_copy(
            src_ref=src, dst_ref=dst, send_sem=send_sem.at[phase, way],
            recv_sem=recv_sem.at[phase, land], device_id=target, device_id_type=MESH,
        )

    def row_copies(phase, send, recv):
        north = remote(send.at[1], recv.at[top_flag], phase, 1, top_flag, north_id)
        south = remote(send.at[0], recv.at[1], phase, 0, 1, south_id)
        return north, south

    def column_copies(phase, send, recv):
        to_west = remote(send.at[pl.ds(0, 8)], recv.at[pl.ds(8, 8)], phase, 2, 2, (lat, west))
        to_east = remote(send.at[pl.ds(8, 8)], recv.at[pl.ds(0, 8)], phase, 3, 3, (lat, east))
        return to_west, to_east

    def start_rows(pair):
        pair[0].start()

        @pl.when(has_south)
        def _():
            pair[1].start()

    def rows_arrive(phase, send, recv):
        remote(send.at[1], recv.at[1], phase, 1, 1, north_id).wait_recv()

        @pl.when(has_south)
        def _():
            remote(send.at[0], recv.at[0], phase, 0, 0, south_id).wait_recv()

    def tile(ref, level, f=0):
        return ref[pl.ds(pl.multiple_of(f * cells + level * ROWS, ROWS), ROWS), :]

    def put(ref, level, value, f=0):
        ref[pl.ds(pl.multiple_of(f * cells + level * ROWS, ROWS), ROWS), :] = value

    for load in loads[:3]:
        load.wait()
    m[...] = mi[...].astype(jnp.float32)
    row_fields = [(t, f * cells) for f in range(nt)] + [(v, 0), (m, 0)]
    pack_rows(row_fields, ns_send, nt * k)
    pl.semaphore_wait(barrier, jnp.where(has_south, 4, 3))
    rows_one = row_copies(0, ns_send, ns_recv)
    start_rows(rows_one)
    loads[3].wait()
    pack_columns([(t, f * cells) for f in range(nt)] + [(u, 0), (m, 0)], ew_send)
    columns_one = column_copies(0, ew_send, ew_recv)
    for copy in columns_one:
        copy.start()
    for load in loads[4:]:
        load.wait()

    bottom = b[...]

    def inner_one(level, carry):
        lower, ratio = carry
        uu, vv, mm = tile(u, level), tile(v, level), tile(m, level)
        speed = 0.5 * (pltpu.roll(uu, 1, 1) + uu)
        is_open = jnp.where(lane == 0, 0.0, mm * pltpu.roll(mm, 1, 1))
        ahead = is_open * (jnp.maximum(speed, 0.0) + lateral_mixing)
        back = is_open * (lateral_mixing - jnp.minimum(speed, 0.0))
        c_west = ahead
        c_east = pltpu.roll(back, COLS - 1, 1)
        c_mid = -(back + pltpu.roll(ahead, COLS - 1, 1))
        speed = 0.5 * (pltpu.roll(vv, 1, 0) + vv)
        is_open = jnp.where(row == 0, 0.0, mm * pltpu.roll(mm, 1, 0))
        ahead = is_open * (jnp.maximum(speed, 0.0) + lateral_mixing)
        back = is_open * (lateral_mixing - jnp.minimum(speed, 0.0))
        c_south = ahead
        c_north = pltpu.roll(back, ROWS - 1, 0)
        c_mid = c_mid - (back + pltpu.roll(ahead, ROWS - 1, 0))
        for i, c in enumerate((c_west, c_east, c_south, c_north, c_mid)):
            put(coef, level, c, i)
        for f in range(nt):
            tt = tile(t, level, f)
            put(s1, level, tt + stencil(tt, c_west, c_east, c_south, c_north, c_mid), f)
        upper = jnp.where(level + 1 < bottom, tile(mix, level), 0.0)
        inverse = 1.0 / (1.0 + lower + upper + lower * ratio)
        ratio = -upper * inverse
        put(solve, level, inverse, 0)
        put(solve, level, ratio, 1)
        put(solve, level, lower * inverse, 2)
        return upper, ratio

    def stencil(tt, c_west, c_east, c_south, c_north, c_mid):
        return (
            (c_west * pltpu.roll(tt, 1, 1) + c_east * pltpu.roll(tt, COLS - 1, 1))
            + (c_south * pltpu.roll(tt, 1, 0) + c_north * pltpu.roll(tt, ROWS - 1, 0))
        ) + c_mid * tt

    zero = jnp.zeros((ROWS, COLS), jnp.float32)
    over_levels(k, inner_one, (zero, zero))

    for copy in columns_one:
        copy.wait_recv()
    unpack_columns(nt + 2, ew_recv)
    rows_arrive(0, ns_send, ns_recv)

    def outer_one(level, carry):
        def line(side, f):
            return ns_recv[side, pl.ds(f * k + level, 1), :]

        uu, vv, mm = tile(u, level), tile(v, level), tile(m, level)
        speed = 0.5 * (tile(y, level, nt) + uu)
        is_open = mm * tile(y, level, nt + 1)
        ahead = is_open * (jnp.maximum(speed, 0.0) + lateral_mixing)
        back = is_open * (lateral_mixing - jnp.minimum(speed, 0.0))
        c_side = jnp.where(lane < COLS // 2, ahead, back)
        c_more = -jnp.where(lane < COLS // 2, back, ahead)
        speed = 0.5 * (line(0, nt) + vv)
        is_open = jnp.where(row == 0, mm * line(0, nt + 1), 0.0)
        c_south = is_open * (jnp.maximum(speed, 0.0) + lateral_mixing)
        c_more = c_more - is_open * (lateral_mixing - jnp.minimum(speed, 0.0))
        speed = 0.5 * (line(1, nt) + vv)
        is_open = jnp.where(row == ROWS - 1, mm * line(1, nt + 1), 0.0)
        c_north = is_open * (lateral_mixing - jnp.minimum(speed, 0.0))
        c_more = c_more - is_open * (jnp.maximum(speed, 0.0) + lateral_mixing)
        put(edge, level, c_side, 0)
        put(edge, level, c_south, 1)
        put(edge, level, c_north, 2)
        put(coef, level, tile(coef, level, 4) + c_more, 4)
        for f in range(nt):
            added = (c_side * tile(y, level, f) + c_more * tile(t, level, f)) + (
                c_south * line(0, f) + c_north * line(1, f)
            )
            put(s1, level, tile(s1, level, f) + added, f)
        return carry

    over_levels(k, outer_one, 0)

    s1_fields = [(s1, f * cells) for f in range(nt)]
    pack_rows(s1_fields, ns_send2, None)
    rows_two = row_copies(1, ns_send2, ns_recv2)
    start_rows(rows_two)
    pack_columns(s1_fields, ew_send2)
    columns_two = column_copies(1, ew_send2, ew_recv2)
    for copy in columns_two:
        copy.start()

    def inner_two(level, carry):
        c = [tile(coef, level, i) for i in range(5)]
        for f in range(nt):
            ss = tile(s1, level, f)
            put(rhs, level, 0.5 * ((tile(t, level, f) + ss) + stencil(ss, *c)), f)
        return carry

    over_levels(k, inner_two, 0)

    for copy in columns_two:
        copy.wait_recv()
    unpack_columns(nt, ew_recv2)
    rows_arrive(1, ns_send2, ns_recv2)

    def forward(level, carry):
        def line(side, f):
            return ns_recv2[side, pl.ds(f * k + level, 1), :]

        c_side, c_south, c_north = (0.5 * tile(edge, level, i) for i in range(3))
        inverse, carried = tile(solve, level, 0), tile(solve, level, 2)
        now = []
        for f in range(nt):
            added = c_side * tile(y, level, f) + (c_south * line(0, f) + c_north * line(1, f))
            value = (tile(rhs, level, f) + added) * inverse + carried * carry[f]
            put(rhs, level, value, f)
            now.append(value)
        return tuple(now)

    over_levels(k, forward, (zero,) * nt)

    def backward(level, carry):
        ratio = tile(solve, level, 1)
        now = []
        for f in range(nt):
            value = tile(rhs, level, f) - ratio * carry[f]
            put(out, level, value, f)
            now.append(value)
        return tuple(now)

    over_levels(k, backward, (zero,) * nt, backward=True)

    for pair in (rows_one, rows_two):
        pair[0].wait_send()
    for copy in columns_one + columns_two:
        copy.wait_send()

    @pl.when(has_south)
    def _():
        rows_one[1].wait_send()
        rows_two[1].wait_send()


def on_device(n_lat, n_lon, tracer, east_vel, north_vel, wet_mask, bottom_level, vertical_mix):
    nt, k, rows, cols = tracer.shape
    cells = k * rows
    f32 = jnp.float32

    def vmem(*shape, dtype=f32):
        return pltpu.VMEM(shape, dtype)

    result = pl.pallas_call(
        functools.partial(kernel, nt, k, n_lat, n_lon),
        out_shape=jax.ShapeDtypeStruct((nt * cells, cols), f32),
        in_specs=[pl.BlockSpec(memory_space=pl.ANY)] * 6,
        out_specs=pl.BlockSpec(memory_space=pltpu.VMEM),
        scratch_shapes=[
            vmem(nt * cells, cols),
            vmem(cells, cols),
            vmem(cells, cols),
            vmem(cells, cols, dtype=jnp.int32),
            vmem(rows, cols, dtype=jnp.int32),
            vmem(cells, cols),
            vmem(cells, cols),
            vmem(nt * cells, cols),
            vmem(nt * cells, cols),
            vmem((nt + 2) * cells, cols),
            vmem(5 * cells, cols),
            vmem(3 * cells, cols),
            vmem(3 * cells, cols),
            vmem(2, (nt + 2) * k, cols),
            vmem(2, (nt + 2) * k, cols),
            vmem(16, cols),
            vmem(16, cols),
            vmem(2, nt * k, cols),
            vmem(2, nt * k, cols),
            vmem(16, cols),
            vmem(16, cols),
            pltpu.SemaphoreType.DMA((6,)),
            pltpu.SemaphoreType.DMA((2, 4)),
            pltpu.SemaphoreType.DMA((2, 4)),
        ],
        compiler_params=pltpu.CompilerParams(
            collective_id=0, has_side_effects=True, vmem_limit_bytes=32 * 1024 * 1024
        ),
    )(
        tracer.reshape(nt * cells, cols),
        east_vel.reshape(cells, cols),
        north_vel.reshape(cells, cols),
        wet_mask.reshape(cells, cols),
        bottom_level,
        vertical_mix.reshape(cells, cols),
    )
    return result.reshape(tracer.shape)


def solution(mesh):
    in_specs = (
        P(None, None, "lat", "lon"),
        P(None, "lat", "lon"),
        P(None, "lat", "lon"),
        P(None, "lat", "lon"),
        P("lat", "lon"),
        P(None, "lat", "lon"),
    )
    out_specs = P(None, None, "lat", "lon")
    return jax.shard_map(
        functools.partial(on_device, mesh.shape["lat"], mesh.shape["lon"]),
        mesh=mesh, in_specs=in_specs, out_specs=out_specs, check_vma=False,
    )
```

```python
import functools

import jax
import jax.numpy as jnp
from jax import lax
from jax.experimental import pallas as pl
from jax.experimental.pallas import tpu as pltpu
from jax.sharding import PartitionSpec as P

lateral_mixing = 0.08
MESH = pl.DeviceIdType.MESH
HIGH = lax.Precision.HIGHEST
ROWS, COLS = 8, 128
UNROLL = 2
GROUPS = 4


def over_levels(count, body, carry, last=None):
    def some(step, carry):
        for part in range(UNROLL):
            level = step * UNROLL + part
            if last is not None:
                level = last - level
            carry = body(level, carry)
        return carry

    return lax.fori_loop(0, count // UNROLL, some, carry)


def kernel(
    nt, k, n_lat, n_lon,
    t_hbm, u_hbm, v_hbm, m_hbm, b_hbm, mix_hbm, out,
    t, u, v, mi, b, mix, m, s1, rhs, y, coef, edge, solve,
    ns_send, ns_recv, ew_send, ew_recv, ns_send2, ns_recv2, ew_send2, ew_recv2,
    load_sem, send_sem, recv_sem, store_sem,
):
    lat, lon = lax.axis_index("lat"), lax.axis_index("lon")
    is_top = lat == n_lat - 1
    has_south = lat > 0
    east = lax.rem(lon + 1, n_lon)
    west = lax.rem(lon + n_lon - 1, n_lon)
    north_id = (jnp.where(is_top, lat, lat + 1), jnp.where(is_top, n_lon - 1 - lon, lon))
    south_id = (jnp.where(has_south, lat - 1, lat), lon)
    top_flag = jnp.where(is_top, 1, 0)
    cells = k * ROWS

    loads = [
        pltpu.make_async_copy(src, dst, load_sem.at[i])
        for i, (src, dst) in enumerate(
            ((t_hbm, t), (v_hbm, v), (m_hbm, mi), (u_hbm, u), (b_hbm, b), (mix_hbm, mix))
        )
    ]
    for load in loads:
        load.start()

    barrier = pltpu.get_barrier_semaphore()
    for target in ((lat, east), (lat, west), north_id):
        pl.semaphore_signal(barrier, inc=1, device_id=target, device_id_type=MESH)

    @pl.when(has_south)
    def _():
        pl.semaphore_signal(barrier, inc=1, device_id=south_id, device_id_type=MESH)

    @pl.when(jnp.logical_not(has_south))
    def _():
        ns_recv[0] = jnp.zeros_like(ns_recv[0])
        ns_recv2[0] = jnp.zeros_like(ns_recv2[0])

    lane = lax.broadcasted_iota(jnp.int32, (ROWS, COLS), 1)
    row = lax.broadcasted_iota(jnp.int32, (ROWS, COLS), 0)
    ends = (lane == 0) | (lane == COLS - 1)

    def pack_rows(fields, send, flip_at):
        for which, at in ((0, 0), (1, ROWS - 1)):
            for f, (ref, base) in enumerate(fields):
                send[which, pl.ds(f * k, k), :] = ref[pl.ds(base + at, k, stride=ROWS), :]

        @pl.when(is_top)
        def _():
            a = lax.broadcasted_iota(jnp.int32, (COLS, COLS), 0)
            c = lax.broadcasted_iota(jnp.int32, (COLS, COLS), 1)
            mirror = jnp.where(a + c == COLS - 1, 1.0, 0.0).astype(jnp.float32)
            turned = jnp.dot(send[1], mirror, precision=HIGH, preferred_element_type=jnp.float32)
            if flip_at is not None:
                at_row = lax.broadcasted_iota(jnp.int32, turned.shape, 0)
                flips = (at_row >= flip_at) & (at_row < flip_at + k)
                turned = jnp.where(flips, -turned, turned)
            send[1] = turned

    def pack_columns(fields, send):
        wide = lax.broadcasted_iota(jnp.int32, (cells, COLS), 1)
        packed = None
        for f, (ref, base) in enumerate(fields):
            moved = pltpu.roll(ref[pl.ds(base, cells), :], 2 * f + 1, 1)
            packed = moved if f == 0 else jnp.where(wide >= 2 * f, moved, packed)
        send[...] = packed.T[:16]

    def unpack_columns(recv):
        at_row = lax.broadcasted_iota(jnp.int32, (16, COLS), 0)
        merged = jnp.where(
            lax.rem(at_row, 2) == 0, pltpu.roll(recv[1], 15, 0), pltpu.roll(recv[0], 1, 0)
        )
        full = jnp.concatenate([merged, jnp.zeros((COLS - 16, COLS), jnp.float32)], axis=0)
        y[...] = full.T

    def side(level, f):
        return pltpu.roll(tile(y, level), COLS - 1 - 2 * f, 1)

    def remote(src, dst, phase, way, land, target):
        return pltpu.make_async_remote_copy(
            src_ref=src, dst_ref=dst, send_sem=send_sem.at[phase, way],
            recv_sem=recv_sem.at[phase, land], device_id=target, device_id_type=MESH,
        )

    def row_copies(phase, send, recv):
        north = remote(send.at[1], recv.at[top_flag], phase, 1, top_flag, north_id)
        south = remote(send.at[0], recv.at[1], phase, 0, 1, south_id)
        return north, south

    def column_copies(phase, send, recv):
        to_west = remote(send, recv.at[1], phase, 2, 2, (lat, west))
        to_east = remote(send, recv.at[0], phase, 3, 3, (lat, east))
        return to_west, to_east

    def start_rows(pair):
        pair[0].start()

        @pl.when(has_south)
        def _():
            pair[1].start()

    def rows_arrive(phase, send, recv):
        remote(send.at[1], recv.at[1], phase, 1, 1, north_id).wait_recv()

        @pl.when(has_south)
        def _():
            remote(send.at[0], recv.at[0], phase, 0, 0, south_id).wait_recv()

    def tile(ref, level, f=0):
        return ref[pl.ds(pl.multiple_of(f * cells + level * ROWS, ROWS), ROWS), :]

    def put(ref, level, value, f=0):
        ref[pl.ds(pl.multiple_of(f * cells + level * ROWS, ROWS), ROWS), :] = value

    def at_level(level):
        return pl.ds(pl.multiple_of(level * ROWS, ROWS), ROWS)

    def tile3(ref, level, f):
        return ref[f, at_level(level), :]

    def put3(ref, level, value, f):
        ref[f, at_level(level), :] = value

    for load in loads[:3]:
        load.wait()
    m[...] = mi[...].astype(jnp.float32)
    row_fields = [(t, f * cells) for f in range(nt)] + [(v, 0), (m, 0)]
    pack_rows(row_fields, ns_send, nt * k)
    loads[3].wait()
    pack_columns([(t, f * cells) for f in range(nt)] + [(u, 0), (m, 0)], ew_send)
    pl.semaphore_wait(barrier, jnp.where(has_south, 4, 3))
    rows_one = row_copies(0, ns_send, ns_recv)
    start_rows(rows_one)
    columns_one = column_copies(0, ew_send, ew_recv)
    for copy in columns_one:
        copy.start()
    for load in loads[4:]:
        load.wait()

    bottom = b[...]

    def inner_one(level, carry):
        lower, ratio = carry
        uu, vv, mm = tile(u, level), tile(v, level), tile(m, level)
        speed = 0.5 * (pltpu.roll(uu, 1, 1) + uu)
        is_open = jnp.where(lane == 0, 0.0, mm * pltpu.roll(mm, 1, 1))
        ahead = is_open * (jnp.maximum(speed, 0.0) + lateral_mixing)
        back = is_open * (lateral_mixing - jnp.minimum(speed, 0.0))
        c_west = ahead
        c_east = pltpu.roll(back, COLS - 1, 1)
        c_mid = -(back + pltpu.roll(ahead, COLS - 1, 1))
        speed = 0.5 * (pltpu.roll(vv, 1, 0) + vv)
        is_open = jnp.where(row == 0, 0.0, mm * pltpu.roll(mm, 1, 0))
        ahead = is_open * (jnp.maximum(speed, 0.0) + lateral_mixing)
        back = is_open * (lateral_mixing - jnp.minimum(speed, 0.0))
        c_south = ahead
        c_north = pltpu.roll(back, ROWS - 1, 0)
        c_mid = c_mid - (back + pltpu.roll(ahead, ROWS - 1, 0))
        for i, c in enumerate((c_west, c_east, c_south, c_north, c_mid)):
            put(coef, level, c, i)
        for f in range(nt):
            tt = tile(t, level, f)
            put(s1, level, tt + stencil(tt, c_west, c_east, c_south, c_north, c_mid), f)
        upper = jnp.where(level + 1 < bottom, tile(mix, level), 0.0)
        inverse = 1.0 / (1.0 + lower + upper + lower * ratio)
        ratio = -upper * inverse
        put(solve, level, inverse, 0)
        put(solve, level, ratio, 1)
        put(solve, level, lower * inverse, 2)
        return upper, ratio

    def stencil(tt, c_west, c_east, c_south, c_north, c_mid):
        return (
            (c_west * pltpu.roll(tt, 1, 1) + c_east * pltpu.roll(tt, COLS - 1, 1))
            + (c_south * pltpu.roll(tt, 1, 0) + c_north * pltpu.roll(tt, ROWS - 1, 0))
        ) + c_mid * tt

    zero = jnp.zeros((ROWS, COLS), jnp.float32)
    over_levels(k, inner_one, (zero, zero))

    for copy in columns_one:
        copy.wait_recv()
    unpack_columns(ew_recv)
    rows_arrive(0, ns_send, ns_recv)

    def outer_one(level, carry):
        def line(which, f):
            return ns_recv[which, pl.ds(f * k + level, 1), :]

        uu, vv, mm = tile(u, level), tile(v, level), tile(m, level)
        speed = 0.5 * (side(level, nt) + uu)
        is_open = jnp.where(ends, mm * side(level, nt + 1), 0.0)
        ahead = is_open * (jnp.maximum(speed, 0.0) + lateral_mixing)
        back = is_open * (lateral_mixing - jnp.minimum(speed, 0.0))
        c_side = jnp.where(lane < COLS // 2, ahead, back)
        c_more = -jnp.where(lane < COLS // 2, back, ahead)
        speed = 0.5 * (line(0, nt) + vv)
        is_open = jnp.where(row == 0, mm * line(0, nt + 1), 0.0)
        c_south = is_open * (jnp.maximum(speed, 0.0) + lateral_mixing)
        c_more = c_more - is_open * (lateral_mixing - jnp.minimum(speed, 0.0))
        speed = 0.5 * (line(1, nt) + vv)
        is_open = jnp.where(row == ROWS - 1, mm * line(1, nt + 1), 0.0)
        c_north = is_open * (lateral_mixing - jnp.minimum(speed, 0.0))
        c_more = c_more - is_open * (jnp.maximum(speed, 0.0) + lateral_mixing)
        put(edge, level, c_side, 0)
        put(edge, level, c_south, 1)
        put(edge, level, c_north, 2)
        put(coef, level, tile(coef, level, 4) + c_more, 4)
        for f in range(nt):
            added = (c_side * side(level, f) + c_more * tile(t, level, f)) + (
                c_south * line(0, f) + c_north * line(1, f)
            )
            put(s1, level, tile(s1, level, f) + added, f)
        return carry

    over_levels(k, outer_one, 0)

    s1_fields = [(s1, f * cells) for f in range(nt)]
    pack_rows(s1_fields, ns_send2, None)
    rows_two = row_copies(1, ns_send2, ns_recv2)
    start_rows(rows_two)
    pack_columns(s1_fields, ew_send2)
    columns_two = column_copies(1, ew_send2, ew_recv2)
    for copy in columns_two:
        copy.start()

    def inner_two(level, carry):
        c = [tile(coef, level, i) for i in range(5)]
        for f in range(nt):
            ss = tile(s1, level, f)
            put3(rhs, level, (tile(t, level, f) + ss) + stencil(ss, *c), f)
        return carry

    over_levels(k, inner_two, 0)

    for copy in columns_two:
        copy.wait_recv()
    unpack_columns(ew_recv2)
    rows_arrive(1, ns_send2, ns_recv2)

    def forward(level, carry):
        def line(which, f):
            return ns_recv2[which, pl.ds(f * k + level, 1), :]

        c_side, c_south, c_north = (tile(edge, level, i) for i in range(3))
        inverse, carried = tile(solve, level, 0), tile(solve, level, 2)
        now = []
        for f in range(nt):
            added = c_side * side(level, f) + (c_south * line(0, f) + c_north * line(1, f))
            value = (tile3(rhs, level, f) + added) * inverse + carried * carry[f]
            put3(rhs, level, value, f)
            now.append(value)
        return tuple(now)

    over_levels(k, forward, (zero,) * nt)

    def backward(level, carry):
        ratio = tile(solve, level, 1)
        now = []
        for f in range(nt):
            value = tile3(rhs, level, f) - ratio * carry[f]
            put3(rhs, level, value, f)
            now.append(value)
        return tuple(now)

    carry = (zero,) * nt
    share = k // GROUPS
    stores = []
    for group in reversed(range(GROUPS)):
        carry = over_levels(share, backward, carry, last=(group + 1) * share - 1)
        span = (slice(None), pl.ds(group * share * ROWS, share * ROWS), slice(None))
        stores.append(pltpu.make_async_copy(rhs.at[span], out.at[span], store_sem.at[group]))
        stores[-1].start()

    for store in stores:
        store.wait()
    for pair in (rows_one, rows_two):
        pair[0].wait_send()
    for copy in columns_one + columns_two:
        copy.wait_send()

    @pl.when(has_south)
    def _():
        rows_one[1].wait_send()
        rows_two[1].wait_send()


def on_device(n_lat, n_lon, tracer, east_vel, north_vel, wet_mask, bottom_level, vertical_mix):
    nt, k, rows, cols = tracer.shape
    cells = k * rows
    f32 = jnp.float32

    def vmem(*shape, dtype=f32):
        return pltpu.VMEM(shape, dtype)

    result = pl.pallas_call(
        functools.partial(kernel, nt, k, n_lat, n_lon),
        out_shape=jax.ShapeDtypeStruct((nt, cells, cols), f32),
        in_specs=[pl.BlockSpec(memory_space=pltpu.HBM)] * 6,
        out_specs=pl.BlockSpec(memory_space=pltpu.HBM),
        scratch_shapes=[
            vmem(nt * cells, cols),
            vmem(cells, cols),
            vmem(cells, cols),
            vmem(cells, cols, dtype=jnp.int32),
            vmem(rows, cols, dtype=jnp.int32),
            vmem(cells, cols),
            vmem(cells, cols),
            vmem(nt * cells, cols),
            vmem(nt, cells, cols),
            vmem(cells, cols),
            vmem(5 * cells, cols),
            vmem(3 * cells, cols),
            vmem(3 * cells, cols),
            vmem(2, (nt + 2) * k, cols),
            vmem(2, (nt + 2) * k, cols),
            vmem(16, cols),
            vmem(2, 16, cols),
            vmem(2, nt * k, cols),
            vmem(2, nt * k, cols),
            vmem(16, cols),
            vmem(2, 16, cols),
            pltpu.SemaphoreType.DMA((6,)),
            pltpu.SemaphoreType.DMA((2, 4)),
            pltpu.SemaphoreType.DMA((2, 4)),
            pltpu.SemaphoreType.DMA((GROUPS,)),
        ],
        compiler_params=pltpu.CompilerParams(
            collective_id=0, has_side_effects=True, vmem_limit_bytes=62 * 1024 * 1024
        ),
    )(
        tracer.reshape(nt * cells, cols),
        east_vel.reshape(cells, cols),
        north_vel.reshape(cells, cols),
        wet_mask.reshape(cells, cols),
        bottom_level,
        vertical_mix.reshape(cells, cols),
    )
    return 0.5 * result.reshape(tracer.shape)


def solution(mesh):
    in_specs = (
        P(None, None, "lat", "lon"),
        P(None, "lat", "lon"),
        P(None, "lat", "lon"),
        P(None, "lat", "lon"),
        P("lat", "lon"),
        P(None, "lat", "lon"),
    )
    out_specs = P(None, None, "lat", "lon")
    return jax.shard_map(
        functools.partial(on_device, mesh.shape["lat"], mesh.shape["lon"]),
        mesh=mesh, in_specs=in_specs, out_specs=out_specs, check_vma=False,
    )
```

```python
import functools

import jax
import jax.numpy as jnp
from jax import lax
from jax.experimental import pallas as pl
from jax.experimental.pallas import tpu as pltpu
from jax.sharding import PartitionSpec as P

lateral_mixing = 0.08
MESH = pl.DeviceIdType.MESH
HIGH = lax.Precision.HIGHEST
ROWS, COLS = 8, 128
GROUPS = 3


def over_levels(count, body, carry, unroll, backward=False):
    def some(step, carry):
        for part in range(unroll):
            level = step * unroll + part
            carry = body(count - 1 - level if backward else level, carry)
        return carry

    if unroll == count:
        return some(0, carry)
    return lax.fori_loop(0, count // unroll, some, carry)


def kernel(
    nt, k, n_lat, n_lon,
    t_hbm, u_hbm, v_hbm, m_hbm, b_hbm, mix_hbm, out,
    t, u, v, mi, b, mix, m, s1, rhs, y, y2, coef, edge, solve,
    ns_send, ns_recv, ew_send, ew_recv, ns_send2, ns_recv2, ew_send2, ew_recv2,
    load_sem, send_sem, recv_sem,
):
    lat, lon = lax.axis_index("lat"), lax.axis_index("lon")
    is_top = lat == n_lat - 1
    has_south = lat > 0
    east = lax.rem(lon + 1, n_lon)
    west = lax.rem(lon + n_lon - 1, n_lon)
    north_id = (jnp.where(is_top, lat, lat + 1), jnp.where(is_top, n_lon - 1 - lon, lon))
    south_id = (jnp.where(has_south, lat - 1, lat), lon)
    top_flag = jnp.where(is_top, 1, 0)
    cells = k * ROWS

    loads = [
        pltpu.make_async_copy(src, dst, load_sem.at[i])
        for i, (src, dst) in enumerate(
            ((t_hbm, t), (v_hbm, v), (m_hbm, mi), (u_hbm, u), (b_hbm, b), (mix_hbm, mix))
        )
    ]
    for load in loads:
        load.start()

    barrier = pltpu.get_barrier_semaphore()
    for target in ((lat, east), (lat, west), north_id):
        pl.semaphore_signal(barrier, inc=1, device_id=target, device_id_type=MESH)

    @pl.when(has_south)
    def _():
        pl.semaphore_signal(barrier, inc=1, device_id=south_id, device_id_type=MESH)

    @pl.when(jnp.logical_not(has_south))
    def _():
        ns_recv[0] = jnp.zeros_like(ns_recv[0])
        ns_recv2[0] = jnp.zeros_like(ns_recv2[0])

    lane = lax.broadcasted_iota(jnp.int32, (ROWS, COLS), 1)
    row = lax.broadcasted_iota(jnp.int32, (ROWS, COLS), 0)
    ends = (lane == 0) | (lane == COLS - 1)

    def pack_rows(fields, send, start, flip):
        for which, at in ((0, 0), (1, ROWS - 1)):
            for f, (ref, base) in enumerate(fields):
                send[which, pl.ds(start + f * k, k), :] = ref[pl.ds(base + at, k, stride=ROWS), :]

        @pl.when(is_top)
        def _():
            a = lax.broadcasted_iota(jnp.int32, (COLS, COLS), 0)
            c = lax.broadcasted_iota(jnp.int32, (COLS, COLS), 1)
            mirror = jnp.where(a + c == COLS - 1, 1.0, 0.0).astype(jnp.float32)
            span = pl.ds(start, len(fields) * k)
            send[1, span, :] = jnp.dot(
                send[1, span, :], mirror, precision=HIGH, preferred_element_type=jnp.float32
            )
            if flip:
                send[1, pl.ds(start, k), :] = -send[1, pl.ds(start, k), :]

    def pack_columns(fields, send):
        wide = lax.broadcasted_iota(jnp.int32, (cells, COLS), 1)
        packed = None
        for f, (ref, base) in enumerate(fields):
            moved = pltpu.roll(ref[pl.ds(base, cells), :], 2 * f + 1, 1)
            packed = moved if f == 0 else jnp.where(wide >= 2 * f, moved, packed)
        send[...] = packed.T[: send.shape[0]]

    def unpack_columns(recv, into):
        lines = recv.shape[1]
        at_row = lax.broadcasted_iota(jnp.int32, (lines, COLS), 0)
        merged = jnp.where(
            lax.rem(at_row, 2) == 0, pltpu.roll(recv[1], lines - 1, 0), pltpu.roll(recv[0], 1, 0)
        )
        full = jnp.concatenate([merged, jnp.zeros((COLS - lines, COLS), jnp.float32)], axis=0)
        into[...] = full.T

    def side(ref, level, f):
        return pltpu.roll(tile(ref, level), COLS - 1 - 2 * f, 1)

    def remote(src, dst, phase, group, way, land, target):
        return pltpu.make_async_remote_copy(
            src_ref=src, dst_ref=dst, send_sem=send_sem.at[phase, group, way],
            recv_sem=recv_sem.at[phase, group, land], device_id=target, device_id_type=MESH,
        )

    def row_copies(phase, group, send, recv, span):
        north = remote(send.at[1, span], recv.at[top_flag, span], phase, group, 1, top_flag, north_id)
        south = remote(send.at[0, span], recv.at[1, span], phase, group, 0, 1, south_id)
        return north, south

    def column_copies(phase, group, send, recv):
        to_west = remote(send, recv.at[1], phase, group, 2, 2, (lat, west))
        to_east = remote(send, recv.at[0], phase, group, 3, 3, (lat, east))
        return to_west, to_east

    def start_rows(pair):
        pair[0].start()

        @pl.when(has_south)
        def _():
            pair[1].start()

    def rows_arrive(phase, group, send, recv, span):
        remote(send.at[1, span], recv.at[1, span], phase, group, 1, 1, north_id).wait_recv()

        @pl.when(has_south)
        def _():
            remote(send.at[0, span], recv.at[0, span], phase, group, 0, 0, south_id).wait_recv()

    per = nt // GROUPS
    groups = range(GROUPS)
    spans_one = [pl.ds(0, (2 + per) * k)] + [pl.ds((2 + g * per) * k, per * k) for g in groups[1:]]
    spans_two = [pl.ds(g * per * k, per * k) for g in groups]

    def place(level, f=0):
        if isinstance(level, int):
            return pl.ds(f * cells + level * ROWS, ROWS)
        return pl.ds(pl.multiple_of(f * cells + level * ROWS, ROWS), ROWS)

    def tile(ref, level, f=0):
        return ref[place(level, f), :]

    def put(ref, level, value, f=0):
        ref[place(level, f), :] = value

    for load in loads[:3]:
        load.wait()
    m[...] = mi[...].astype(jnp.float32)
    rows_one = []
    for g in groups:
        fields = [(t, f * cells) for f in range(g * per, (g + 1) * per)]
        if g == 0:
            fields = [(v, 0), (m, 0)] + fields
        pack_rows(fields, ns_send, spans_one[g].start, g == 0)
        if g == 0:
            pl.semaphore_wait(barrier, jnp.where(has_south, 4, 3))
        rows_one.append(row_copies(0, g, ns_send, ns_recv, spans_one[g]))
        start_rows(rows_one[g])
        if g == 0:
            loads[3].wait()
            pack_columns([(t, f * cells) for f in range(nt)] + [(u, 0), (m, 0)], ew_send)
            columns_one = column_copies(0, 0, ew_send, ew_recv)
            for copy in columns_one:
                copy.start()
    for load in loads[4:]:
        load.wait()

    bottom = b[...]

    def inner_one(level, carry):
        lower, ratio = carry
        uu, vv, mm = tile(u, level), tile(v, level), tile(m, level)
        speed = 0.5 * (pltpu.roll(uu, 1, 1) + uu)
        is_open = jnp.where(lane == 0, 0.0, mm * pltpu.roll(mm, 1, 1))
        ahead = is_open * (jnp.maximum(speed, 0.0) + lateral_mixing)
        back = is_open * (lateral_mixing - jnp.minimum(speed, 0.0))
        c_west = ahead
        c_east = pltpu.roll(back, COLS - 1, 1)
        c_mid = -(back + pltpu.roll(ahead, COLS - 1, 1))
        speed = 0.5 * (pltpu.roll(vv, 1, 0) + vv)
        is_open = jnp.where(row == 0, 0.0, mm * pltpu.roll(mm, 1, 0))
        ahead = is_open * (jnp.maximum(speed, 0.0) + lateral_mixing)
        back = is_open * (lateral_mixing - jnp.minimum(speed, 0.0))
        c_south = ahead
        c_north = pltpu.roll(back, ROWS - 1, 0)
        c_mid = c_mid - (back + pltpu.roll(ahead, ROWS - 1, 0))
        for i, c in enumerate((c_west, c_east, c_south, c_north, c_mid)):
            put(coef, level, c, i)
        for f in range(nt):
            tt = tile(t, level, f)
            put(s1, level, tt + stencil(tt, c_west, c_east, c_south, c_north, c_mid), f)
        upper = jnp.where(level + 1 < bottom, tile(mix, level), 0.0)
        inverse = 1.0 / (1.0 + lower + upper + lower * ratio)
        ratio = -upper * inverse
        put(solve, level, inverse, 0)
        put(solve, level, ratio, 1)
        put(solve, level, lower * inverse, 2)
        return upper, ratio

    def stencil(tt, c_west, c_east, c_south, c_north, c_mid):
        return (
            (c_west * pltpu.roll(tt, 1, 1) + c_east * pltpu.roll(tt, COLS - 1, 1))
            + (c_south * pltpu.roll(tt, 1, 0) + c_north * pltpu.roll(tt, ROWS - 1, 0))
        ) + c_mid * tt

    zero = jnp.zeros((ROWS, COLS), jnp.float32)
    over_levels(k, inner_one, (zero, zero), 4)

    for copy in columns_one:
        copy.wait_recv()
    unpack_columns(ew_recv, y)

    def line(which, level, f):
        return ns_recv[which, pl.ds((2 + f) * k + level, 1), :]

    def outer_faces(level, carry):
        uu, vv, mm = tile(u, level), tile(v, level), tile(m, level)
        speed = 0.5 * (side(y, level, nt) + uu)
        is_open = jnp.where(ends, mm * side(y, level, nt + 1), 0.0)
        ahead = is_open * (jnp.maximum(speed, 0.0) + lateral_mixing)
        back = is_open * (lateral_mixing - jnp.minimum(speed, 0.0))
        c_side = jnp.where(lane < COLS // 2, ahead, back)
        c_more = -jnp.where(lane < COLS // 2, back, ahead)
        speed = 0.5 * (line(0, level, -2) + vv)
        is_open = jnp.where(row == 0, mm * line(0, level, -1), 0.0)
        c_south = is_open * (jnp.maximum(speed, 0.0) + lateral_mixing)
        c_more = c_more - is_open * (lateral_mixing - jnp.minimum(speed, 0.0))
        speed = 0.5 * (line(1, level, -2) + vv)
        is_open = jnp.where(row == ROWS - 1, mm * line(1, level, -1), 0.0)
        c_north = is_open * (lateral_mixing - jnp.minimum(speed, 0.0))
        c_more = c_more - is_open * (jnp.maximum(speed, 0.0) + lateral_mixing)
        for i, c in enumerate((c_side, c_south, c_north, c_more)):
            put(edge, level, c, i)
        put(coef, level, tile(coef, level, 4) + c_more, 4)
        return carry

    rows_two, columns_two = [], []
    for g in groups:
        mine = range(g * per, (g + 1) * per)

        def outer_one(level, carry):
            c_side, c_south, c_north, c_more = (tile(edge, level, i) for i in range(4))
            for f in mine:
                added = (c_side * side(y, level, f) + c_more * tile(t, level, f)) + (
                    c_south * line(0, level, f) + c_north * line(1, level, f)
                )
                put(s1, level, tile(s1, level, f) + added, f)
            return carry

        def inner_two(level, carry):
            c = [tile(coef, level, i) for i in range(5)]
            for f in mine:
                ss = tile(s1, level, f)
                put(rhs, level, 0.5 * ((tile(t, level, f) + ss) + stencil(ss, *c)), f)
            return carry

        rows_arrive(0, g, ns_send, ns_recv, spans_one[g])
        if g == 0:
            over_levels(k, outer_faces, 0, 8)
        over_levels(k, outer_one, 0, k)
        fields = [(s1, f * cells) for f in mine]
        pack_rows(fields, ns_send2, g * per * k, False)
        rows_two.append(row_copies(1, g, ns_send2, ns_recv2, spans_two[g]))
        start_rows(rows_two[g])
        pack_columns(fields, ew_send2.at[g])
        columns_two.append(column_copies(1, g, ew_send2.at[g], ew_recv2.at[g]))
        for copy in columns_two[g]:
            copy.start()
        over_levels(k, inner_two, 0, 8)

    for g in groups:
        mine = range(g * per, (g + 1) * per)
        sides = y2.at[g]

        def forward(level, carry):
            c_side, c_south, c_north = (0.5 * tile(edge, level, i) for i in range(3))
            inverse, carried = tile(solve, level, 0), tile(solve, level, 2)
            now = []
            for i, f in enumerate(mine):
                south = ns_recv2[0, pl.ds(f * k + level, 1), :]
                north = ns_recv2[1, pl.ds(f * k + level, 1), :]
                added = c_side * side(sides, level, i) + (c_south * south + c_north * north)
                value = (tile(rhs, level, f) + added) * inverse + carried * carry[i]
                put(rhs, level, value, f)
                now.append(value)
            return tuple(now)

        def backward(level, carry):
            ratio = tile(solve, level, 1)
            now = []
            for i, f in enumerate(mine):
                value = tile(rhs, level, f) - ratio * carry[i]
                put(out, level, value, f)
                now.append(value)
            return tuple(now)

        for copy in columns_two[g]:
            copy.wait_recv()
        unpack_columns(ew_recv2.at[g], sides)
        rows_arrive(1, g, ns_send2, ns_recv2, spans_two[g])
        over_levels(k, forward, (zero,) * per, k)
        over_levels(k, backward, (zero,) * per, k, backward=True)

    for copy in columns_one:
        copy.wait_send()
    for g in groups:
        rows_one[g][0].wait_send()
        rows_two[g][0].wait_send()
        for copy in columns_two[g]:
            copy.wait_send()

    @pl.when(has_south)
    def _():
        for pair in rows_one + rows_two:
            pair[1].wait_send()


def on_device(n_lat, n_lon, tracer, east_vel, north_vel, wet_mask, bottom_level, vertical_mix):
    nt, k, rows, cols = tracer.shape
    cells = k * rows
    f32 = jnp.float32

    def vmem(*shape, dtype=f32):
        return pltpu.VMEM(shape, dtype)

    result = pl.pallas_call(
        functools.partial(kernel, nt, k, n_lat, n_lon),
        out_shape=pltpu.VMEM((nt * cells, cols), f32),
        in_specs=[pl.BlockSpec(memory_space=pltpu.HBM)] * 6,
        out_specs=pl.BlockSpec(memory_space=pltpu.VMEM),
        scratch_shapes=[
            vmem(nt * cells, cols),
            vmem(cells, cols),
            vmem(cells, cols),
            vmem(cells, cols, dtype=jnp.int32),
            vmem(rows, cols, dtype=jnp.int32),
            vmem(cells, cols),
            vmem(cells, cols),
            vmem(nt * cells, cols),
            vmem(nt * cells, cols),
            vmem(cells, cols),
            vmem(GROUPS, cells, cols),
            vmem(5 * cells, cols),
            vmem(4 * cells, cols),
            vmem(3 * cells, cols),
            vmem(2, (nt + 2) * k, cols),
            vmem(2, (nt + 2) * k, cols),
            vmem(16, cols),
            vmem(2, 16, cols),
            vmem(2, nt * k, cols),
            vmem(2, nt * k, cols),
            vmem(GROUPS, 8, cols),
            vmem(GROUPS, 2, 8, cols),
            pltpu.SemaphoreType.DMA((6,)),
            pltpu.SemaphoreType.DMA((2, GROUPS, 4)),
            pltpu.SemaphoreType.DMA((2, GROUPS, 4)),
        ],
        compiler_params=pltpu.CompilerParams(
            collective_id=0, has_side_effects=True, vmem_limit_bytes=62 * 1024 * 1024
        ),
    )(
        tracer.reshape(nt * cells, cols),
        east_vel.reshape(cells, cols),
        north_vel.reshape(cells, cols),
        wet_mask.reshape(cells, cols),
        bottom_level,
        vertical_mix.reshape(cells, cols),
    )
    return result.reshape(tracer.shape)


def solution(mesh):
    in_specs = (
        P(None, None, "lat", "lon"),
        P(None, "lat", "lon"),
        P(None, "lat", "lon"),
        P(None, "lat", "lon"),
        P("lat", "lon"),
        P(None, "lat", "lon"),
    )
    out_specs = P(None, None, "lat", "lon")
    return jax.shard_map(
        functools.partial(on_device, mesh.shape["lat"], mesh.shape["lon"]),
        mesh=mesh, in_specs=in_specs, out_specs=out_specs, check_vma=False,
    )
```

```python
import functools

import jax
import jax.numpy as jnp
from jax import lax
from jax.experimental import pallas as pl
from jax.experimental.pallas import tpu as pltpu
from jax.sharding import PartitionSpec as P

lateral_mixing = 0.08
MESH = pl.DeviceIdType.MESH
ROWS, COLS = 8, 128
GROUPS = 3


def over_levels(count, body, carry, unroll, backward=False):
    def some(step, carry):
        for part in range(unroll):
            level = step * unroll + part
            carry = body(count - 1 - level if backward else level, carry)
        return carry

    if unroll == count:
        return some(0, carry)
    return lax.fori_loop(0, count // unroll, some, carry)


def kernel(
    nt, k, n_lat, n_lon,
    t_hbm, u_hbm, v_hbm, m_hbm, b_hbm, mix_hbm, out,
    t, u, v, mi, b, mix, m, s1, rhs, y, y2, coef, edge, solve,
    ns_send, ns_recv, ew_send, ew_recv, ns_send2, ns_recv2, ew_send2, ew_recv2,
    load_sem, send_sem, recv_sem,
):
    lat, lon = lax.axis_index("lat"), lax.axis_index("lon")
    is_top = lat == n_lat - 1
    has_south = lat > 0
    east = lax.rem(lon + 1, n_lon)
    west = lax.rem(lon + n_lon - 1, n_lon)
    north_id = (jnp.where(is_top, lat, lat + 1), jnp.where(is_top, n_lon - 1 - lon, lon))
    south_id = (jnp.where(has_south, lat - 1, lat), lon)
    top_flag = jnp.where(is_top, 1, 0)
    cells = k * ROWS

    loads = [
        pltpu.make_async_copy(src, dst, load_sem.at[i])
        for i, (src, dst) in enumerate(
            ((t_hbm, t), (v_hbm, v), (m_hbm, mi), (u_hbm, u), (b_hbm, b), (mix_hbm, mix))
        )
    ]
    for load in loads:
        load.start()

    barrier = pltpu.get_barrier_semaphore()
    for target in ((lat, east), (lat, west), north_id):
        pl.semaphore_signal(barrier, inc=1, device_id=target, device_id_type=MESH)

    @pl.when(has_south)
    def _():
        pl.semaphore_signal(barrier, inc=1, device_id=south_id, device_id_type=MESH)

    @pl.when(jnp.logical_not(has_south))
    def _():
        ns_recv[0] = jnp.zeros_like(ns_recv[0])
        ns_recv2[0] = jnp.zeros_like(ns_recv2[0])

    lane = lax.broadcasted_iota(jnp.int32, (ROWS, COLS), 1)
    row = lax.broadcasted_iota(jnp.int32, (ROWS, COLS), 0)
    ends = (lane == 0) | (lane == COLS - 1)

    def pack_rows(fields, send, start, flip):
        for which, at in ((0, 0), (1, ROWS - 1)):
            for f, (ref, base) in enumerate(fields):
                send[which, pl.ds(start + f * k, k), :] = ref[pl.ds(base + at, k, stride=ROWS), :]

        @pl.when(is_top)
        def _():
            a = lax.broadcasted_iota(jnp.int32, (COLS, COLS), 0)
            c = lax.broadcasted_iota(jnp.int32, (COLS, COLS), 1)
            mirror = jnp.where(a + c == COLS - 1, 1.0, 0.0).astype(jnp.bfloat16)
            span = pl.ds(start, len(fields) * k)
            rest = send[1, span, :]
            turned = None
            for _ in range(3):
                piece = rest.astype(jnp.bfloat16)
                rest = rest - piece.astype(jnp.float32)
                part = jnp.dot(piece, mirror, preferred_element_type=jnp.float32)
                turned = part if turned is None else turned + part
            send[1, span, :] = turned
            if flip:
                send[1, pl.ds(start, k), :] = -send[1, pl.ds(start, k), :]

    each = COLS // (2 * k)

    def pack_columns(fields, send):
        for block in range(send.shape[0]):
            packed = None
            for f, (ref, base) in enumerate(fields[block * each : (block + 1) * each]):
                for level in range(k):
                    at = 2 * (f * k + level)
                    moved = pltpu.roll(ref[pl.ds(base + level * ROWS, ROWS), :], at + 1, 1)
                    packed = moved if at == 0 else jnp.where(lane >= at, moved, packed)
            send[block] = packed

    def unpack_columns(recv, into):
        for block in range(recv.shape[1]):
            into[block] = jnp.where(
                lax.rem(lane, 2) == 0,
                pltpu.roll(recv[1, block], COLS - 1, 1),
                pltpu.roll(recv[0, block], 1, 1),
            )

    def side(ref, level, f):
        return pltpu.roll(ref[f // each], COLS - 1 - 2 * (f % each * k + level), 1)

    def remote(src, dst, phase, group, way, land, target):
        return pltpu.make_async_remote_copy(
            src_ref=src, dst_ref=dst, send_sem=send_sem.at[phase, group, way],
            recv_sem=recv_sem.at[phase, group, land], device_id=target, device_id_type=MESH,
        )

    def row_copies(phase, group, send, recv, span):
        north = remote(send.at[1, span], recv.at[top_flag, span], phase, group, 1, top_flag, north_id)
        south = remote(send.at[0, span], recv.at[1, span], phase, group, 0, 1, south_id)
        return north, south

    def column_copies(phase, group, send, recv):
        to_west = remote(send, recv.at[1], phase, group, 2, 2, (lat, west))
        to_east = remote(send, recv.at[0], phase, group, 3, 3, (lat, east))
        return to_west, to_east

    def start_rows(pair):
        pair[0].start()

        @pl.when(has_south)
        def _():
            pair[1].start()

    def rows_arrive(phase, group, send, recv, span):
        remote(send.at[1, span], recv.at[1, span], phase, group, 1, 1, north_id).wait_recv()

        @pl.when(has_south)
        def _():
            remote(send.at[0, span], recv.at[0, span], phase, group, 0, 0, south_id).wait_recv()

    per = nt // GROUPS
    groups = range(GROUPS)
    spans_one = [pl.ds(0, (2 + per) * k)] + [pl.ds((2 + g * per) * k, per * k) for g in groups[1:]]
    spans_two = [pl.ds(g * per * k, per * k) for g in groups]

    def place(level, f=0):
        if isinstance(level, int):
            return pl.ds(f * cells + level * ROWS, ROWS)
        return pl.ds(pl.multiple_of(f * cells + level * ROWS, ROWS), ROWS)

    def tile(ref, level, f=0):
        return ref[place(level, f), :]

    def put(ref, level, value, f=0):
        ref[place(level, f), :] = value

    for load in loads[:3]:
        load.wait()
    m[...] = mi[...].astype(jnp.float32)
    rows_one = []
    for g in groups:
        fields = [(t, f * cells) for f in range(g * per, (g + 1) * per)]
        if g == 0:
            fields = [(v, 0), (m, 0)] + fields
        pack_rows(fields, ns_send, spans_one[g].start, g == 0)
        if g == 0:
            pl.semaphore_wait(barrier, jnp.where(has_south, 4, 3))
        rows_one.append(row_copies(0, g, ns_send, ns_recv, spans_one[g]))
        start_rows(rows_one[g])
        if g == 0:
            loads[3].wait()
            pack_columns([(t, f * cells) for f in range(nt)] + [(u, 0), (m, 0)], ew_send)
            columns_one = column_copies(0, 0, ew_send, ew_recv)
            for copy in columns_one:
                copy.start()
    for load in loads[4:]:
        load.wait()

    bottom = b[...]

    def inner_one(level, carry):
        lower, ratio = carry
        uu, vv, mm = tile(u, level), tile(v, level), tile(m, level)
        speed = 0.5 * (pltpu.roll(uu, 1, 1) + uu)
        is_open = jnp.where(lane == 0, 0.0, mm * pltpu.roll(mm, 1, 1))
        ahead = is_open * (jnp.maximum(speed, 0.0) + lateral_mixing)
        back = is_open * (lateral_mixing - jnp.minimum(speed, 0.0))
        c_west = ahead
        c_east = pltpu.roll(back, COLS - 1, 1)
        c_mid = -(back + pltpu.roll(ahead, COLS - 1, 1))
        speed = 0.5 * (pltpu.roll(vv, 1, 0) + vv)
        is_open = jnp.where(row == 0, 0.0, mm * pltpu.roll(mm, 1, 0))
        ahead = is_open * (jnp.maximum(speed, 0.0) + lateral_mixing)
        back = is_open * (lateral_mixing - jnp.minimum(speed, 0.0))
        c_south = ahead
        c_north = pltpu.roll(back, ROWS - 1, 0)
        c_mid = c_mid - (back + pltpu.roll(ahead, ROWS - 1, 0))
        for i, c in enumerate((c_west, c_east, c_south, c_north, c_mid)):
            put(coef, level, c, i)
        for f in range(nt):
            tt = tile(t, level, f)
            put(s1, level, tt + stencil(tt, c_west, c_east, c_south, c_north, c_mid), f)
        upper = jnp.where(level + 1 < bottom, tile(mix, level), 0.0)
        inverse = 1.0 / (1.0 + lower + upper + lower * ratio)
        ratio = -upper * inverse
        put(solve, level, inverse, 0)
        put(solve, level, ratio, 1)
        put(solve, level, lower * inverse, 2)
        return upper, ratio

    def stencil(tt, c_west, c_east, c_south, c_north, c_mid):
        return (
            (c_west * pltpu.roll(tt, 1, 1) + c_east * pltpu.roll(tt, COLS - 1, 1))
            + (c_south * pltpu.roll(tt, 1, 0) + c_north * pltpu.roll(tt, ROWS - 1, 0))
        ) + c_mid * tt

    zero = jnp.zeros((ROWS, COLS), jnp.float32)
    over_levels(k, inner_one, (zero, zero), 4)

    for copy in columns_one:
        copy.wait_recv()
    unpack_columns(ew_recv, y)

    def line(which, level, f):
        return ns_recv[which, pl.ds((2 + f) * k + level, 1), :]

    def outer_faces(level, carry):
        uu, vv, mm = tile(u, level), tile(v, level), tile(m, level)
        speed = 0.5 * (side(y, level, nt) + uu)
        is_open = jnp.where(ends, mm * side(y, level, nt + 1), 0.0)
        ahead = is_open * (jnp.maximum(speed, 0.0) + lateral_mixing)
        back = is_open * (lateral_mixing - jnp.minimum(speed, 0.0))
        c_side = jnp.where(lane < COLS // 2, ahead, back)
        c_more = -jnp.where(lane < COLS // 2, back, ahead)
        speed = 0.5 * (line(0, level, -2) + vv)
        is_open = jnp.where(row == 0, mm * line(0, level, -1), 0.0)
        c_south = is_open * (jnp.maximum(speed, 0.0) + lateral_mixing)
        c_more = c_more - is_open * (lateral_mixing - jnp.minimum(speed, 0.0))
        speed = 0.5 * (line(1, level, -2) + vv)
        is_open = jnp.where(row == ROWS - 1, mm * line(1, level, -1), 0.0)
        c_north = is_open * (lateral_mixing - jnp.minimum(speed, 0.0))
        c_more = c_more - is_open * (jnp.maximum(speed, 0.0) + lateral_mixing)
        for i, c in enumerate((c_side, c_south, c_north, c_more)):
            put(edge, level, c, i)
        put(coef, level, tile(coef, level, 4) + c_more, 4)
        return carry

    rows_two, columns_two = [], []
    for g in groups:
        mine = range(g * per, (g + 1) * per)

        def outer_one(level, carry):
            c_side, c_south, c_north, c_more = (tile(edge, level, i) for i in range(4))
            for f in mine:
                added = (c_side * side(y, level, f) + c_more * tile(t, level, f)) + (
                    c_south * line(0, level, f) + c_north * line(1, level, f)
                )
                put(s1, level, tile(s1, level, f) + added, f)
            return carry

        def inner_two(level, carry):
            c = [tile(coef, level, i) for i in range(5)]
            for f in mine:
                ss = tile(s1, level, f)
                put(rhs, level, 0.5 * ((tile(t, level, f) + ss) + stencil(ss, *c)), f)
            return carry

        rows_arrive(0, g, ns_send, ns_recv, spans_one[g])
        if g == 0:
            over_levels(k, outer_faces, 0, k)
        over_levels(k, outer_one, 0, k)
        fields = [(s1, f * cells) for f in mine]
        pack_rows(fields, ns_send2, g * per * k, False)
        rows_two.append(row_copies(1, g, ns_send2, ns_recv2, spans_two[g]))
        start_rows(rows_two[g])
        pack_columns(fields, ew_send2.at[g])
        columns_two.append(column_copies(1, g, ew_send2.at[g], ew_recv2.at[g]))
        for copy in columns_two[g]:
            copy.start()
        over_levels(k, inner_two, 0, 8)

    for g in groups:
        mine = range(g * per, (g + 1) * per)
        sides = y2.at[g]

        def forward(level, carry):
            c_side, c_south, c_north = (0.5 * tile(edge, level, i) for i in range(3))
            inverse, carried = tile(solve, level, 0), tile(solve, level, 2)
            now = []
            for i, f in enumerate(mine):
                south = ns_recv2[0, pl.ds(f * k + level, 1), :]
                north = ns_recv2[1, pl.ds(f * k + level, 1), :]
                added = c_side * side(sides, level, i) + (c_south * south + c_north * north)
                value = (tile(rhs, level, f) + added) * inverse + carried * carry[i]
                put(rhs, level, value, f)
                now.append(value)
            return tuple(now)

        def backward(level, carry):
            ratio = tile(solve, level, 1)
            now = []
            for i, f in enumerate(mine):
                value = tile(rhs, level, f) - ratio * carry[i]
                put(out, level, value, f)
                now.append(value)
            return tuple(now)

        for copy in columns_two[g]:
            copy.wait_recv()
        unpack_columns(ew_recv2.at[g], sides)
        rows_arrive(1, g, ns_send2, ns_recv2, spans_two[g])
        over_levels(k, forward, (zero,) * per, k)
        over_levels(k, backward, (zero,) * per, k, backward=True)

    for copy in columns_one:
        copy.wait_send()
    for g in groups:
        rows_one[g][0].wait_send()
        rows_two[g][0].wait_send()
        for copy in columns_two[g]:
            copy.wait_send()

    @pl.when(has_south)
    def _():
        for pair in rows_one + rows_two:
            pair[1].wait_send()


def on_device(n_lat, n_lon, tracer, east_vel, north_vel, wet_mask, bottom_level, vertical_mix):
    nt, k, rows, cols = tracer.shape
    cells = k * rows
    f32 = jnp.float32
    blocks = (nt + 2) * k * 2 // cols

    def vmem(*shape, dtype=f32):
        return pltpu.VMEM(shape, dtype)

    result = pl.pallas_call(
        functools.partial(kernel, nt, k, n_lat, n_lon),
        out_shape=pltpu.VMEM((nt * cells, cols), f32),
        in_specs=[pl.BlockSpec(memory_space=pltpu.HBM)] * 6,
        out_specs=pl.BlockSpec(memory_space=pltpu.VMEM),
        scratch_shapes=[
            vmem(nt * cells, cols),
            vmem(cells, cols),
            vmem(cells, cols),
            vmem(cells, cols, dtype=jnp.int32),
            vmem(rows, cols, dtype=jnp.int32),
            vmem(cells, cols),
            vmem(cells, cols),
            vmem(nt * cells, cols),
            vmem(nt * cells, cols),
            vmem(blocks, rows, cols),
            vmem(GROUPS, 1, rows, cols),
            vmem(5 * cells, cols),
            vmem(4 * cells, cols),
            vmem(3 * cells, cols),
            vmem(2, (nt + 2) * k, cols),
            vmem(2, (nt + 2) * k, cols),
            vmem(blocks, rows, cols),
            vmem(2, blocks, rows, cols),
            vmem(2, nt * k, cols),
            vmem(2, nt * k, cols),
            vmem(GROUPS, 1, rows, cols),
            vmem(GROUPS, 2, 1, rows, cols),
            pltpu.SemaphoreType.DMA((6,)),
            pltpu.SemaphoreType.DMA((2, GROUPS, 4)),
            pltpu.SemaphoreType.DMA((2, GROUPS, 4)),
        ],
        compiler_params=pltpu.CompilerParams(
            collective_id=0, has_side_effects=True, vmem_limit_bytes=62 * 1024 * 1024
        ),
    )(
        tracer.reshape(nt * cells, cols),
        east_vel.reshape(cells, cols),
        north_vel.reshape(cells, cols),
        wet_mask.reshape(cells, cols),
        bottom_level,
        vertical_mix.reshape(cells, cols),
    )
    return result.reshape(tracer.shape)


def solution(mesh):
    in_specs = (
        P(None, None, "lat", "lon"),
        P(None, "lat", "lon"),
        P(None, "lat", "lon"),
        P(None, "lat", "lon"),
        P("lat", "lon"),
        P(None, "lat", "lon"),
    )
    out_specs = P(None, None, "lat", "lon")
    return jax.shard_map(
        functools.partial(on_device, mesh.shape["lat"], mesh.shape["lon"]),
        mesh=mesh, in_specs=in_specs, out_specs=out_specs, check_vma=False,
    )
```

```python
import functools

import jax
import jax.numpy as jnp
from jax import lax
from jax.experimental import pallas as pl
from jax.experimental.pallas import tpu as pltpu
from jax.sharding import PartitionSpec as P

lateral_mixing = 0.08
MESH = pl.DeviceIdType.MESH
ROWS, COLS = 8, 128
GROUPS = 3


def over_levels(count, body, carry, unroll, backward=False):
    def some(step, carry):
        for part in range(unroll):
            level = step * unroll + part
            carry = body(count - 1 - level if backward else level, carry)
        return carry

    if unroll == count:
        return some(0, carry)
    return lax.fori_loop(0, count // unroll, some, carry)


def kernel(
    nt, k, n_lat, n_lon,
    t_hbm, u_hbm, v_hbm, m_hbm, b_hbm, mix_hbm, t_rows, v_rows, m_rows, out,
    t, u, v, mi, b, mix, m, s1, rhs, y, y2, coef, edge, solve,
    ns_recv, mask_recv, wide_mask, ew_send, ew_recv, ns_send2, ns_recv2, ew_send2, ew_recv2,
    load_sem, send_sem, recv_sem,
):
    lat, lon = lax.axis_index("lat"), lax.axis_index("lon")
    is_top = lat == n_lat - 1
    has_south = lat > 0
    east = lax.rem(lon + 1, n_lon)
    west = lax.rem(lon + n_lon - 1, n_lon)
    north_id = (jnp.where(is_top, lat, lat + 1), jnp.where(is_top, n_lon - 1 - lon, lon))
    south_id = (jnp.where(has_south, lat - 1, lat), lon)
    top_flag = jnp.where(is_top, 1, 0)
    cells = k * ROWS

    loads = [
        pltpu.make_async_copy(src, dst, load_sem.at[i])
        for i, (src, dst) in enumerate(
            ((t_hbm, t), (v_hbm, v), (m_hbm, mi), (u_hbm, u), (b_hbm, b), (mix_hbm, mix))
        )
    ]
    for load in loads:
        load.start()

    barrier = pltpu.get_barrier_semaphore()
    for target in ((lat, east), (lat, west), north_id):
        pl.semaphore_signal(barrier, inc=1, device_id=target, device_id_type=MESH)

    @pl.when(has_south)
    def _():
        pl.semaphore_signal(barrier, inc=1, device_id=south_id, device_id_type=MESH)

    @pl.when(jnp.logical_not(has_south))
    def _():
        ns_recv[0] = jnp.zeros_like(ns_recv[0])
        ns_recv2[0] = jnp.zeros_like(ns_recv2[0])
        mask_recv[0] = jnp.zeros_like(mask_recv[0])

    lane = lax.broadcasted_iota(jnp.int32, (ROWS, COLS), 1)
    row = lax.broadcasted_iota(jnp.int32, (ROWS, COLS), 0)
    ends = (lane == 0) | (lane == COLS - 1)

    def pack_rows(fields, send, start):
        for which, at in ((0, 0), (1, ROWS - 1)):
            for f, (ref, base) in enumerate(fields):
                send[which, pl.ds(start + f * k, k), :] = ref[pl.ds(base + at, k, stride=ROWS), :]

    def mirrored(rest):
        a = lax.broadcasted_iota(jnp.int32, (COLS, COLS), 0)
        c = lax.broadcasted_iota(jnp.int32, (COLS, COLS), 1)
        mirror = jnp.where(a + c == COLS - 1, 1.0, 0.0).astype(jnp.bfloat16)
        turned = None
        for _ in range(3):
            piece = rest.astype(jnp.bfloat16)
            rest = rest - piece.astype(jnp.float32)
            part = jnp.dot(piece, mirror, preferred_element_type=jnp.float32)
            turned = part if turned is None else turned + part
        return turned

    def fold_rows(recv, start, count, flip=False):
        @pl.when(is_top)
        def _():
            span = pl.ds(start, count)
            turned = mirrored(recv[1, span, :])
            recv[1, span, :] = -turned if flip else turned

    each = COLS // (2 * k)

    def pack_columns(fields, send):
        for block in range(send.shape[0]):
            packed = None
            for f, (ref, base) in enumerate(fields[block * each : (block + 1) * each]):
                for level in range(k):
                    at = 2 * (f * k + level)
                    moved = pltpu.roll(ref[pl.ds(base + level * ROWS, ROWS), :], at + 1, 1)
                    packed = moved if at == 0 else jnp.where(lane >= at, moved, packed)
            send[block] = packed

    def unpack_columns(recv, into):
        for block in range(recv.shape[1]):
            into[block] = jnp.where(
                lax.rem(lane, 2) == 0,
                pltpu.roll(recv[1, block], COLS - 1, 1),
                pltpu.roll(recv[0, block], 1, 1),
            )

    def side(ref, level, f):
        return pltpu.roll(ref[f // each], COLS - 1 - 2 * (f % each * k + level), 1)

    def remote(src, dst, phase, group, way, land, target):
        return pltpu.make_async_remote_copy(
            src_ref=src, dst_ref=dst, send_sem=send_sem.at[phase, group, way],
            recv_sem=recv_sem.at[phase, group, land], device_id=target, device_id_type=MESH,
        )

    def row_copies(phase, group, south_src, north_src, recv, span):
        north = remote(north_src, recv.at[top_flag, span], phase, group, 1, top_flag, north_id)
        south = remote(south_src, recv.at[1, span], phase, group, 0, 1, south_id)
        return north, south

    def column_copies(phase, group, send, recv):
        to_west = remote(send, recv.at[1], phase, group, 2, 2, (lat, west))
        to_east = remote(send, recv.at[0], phase, group, 3, 3, (lat, east))
        return to_west, to_east

    def start_rows(pair):
        pair[0].start()

        @pl.when(has_south)
        def _():
            pair[1].start()

    def rows_arrive(phase, group, south_src, north_src, recv, span):
        remote(north_src, recv.at[1, span], phase, group, 1, 1, north_id).wait_recv()

        @pl.when(has_south)
        def _():
            remote(south_src, recv.at[0, span], phase, group, 0, 0, south_id).wait_recv()

    per = nt // GROUPS
    groups = range(GROUPS)
    spans = [pl.ds(g * per * k, per * k) for g in groups]

    def place(level, f=0):
        if isinstance(level, int):
            return pl.ds(f * cells + level * ROWS, ROWS)
        return pl.ds(pl.multiple_of(f * cells + level * ROWS, ROWS), ROWS)

    def tile(ref, level, f=0):
        return ref[place(level, f), :]

    def put(ref, level, value, f=0):
        ref[place(level, f), :] = value

    sources = [(v_rows.at[:, 0, :], v_rows.at[:, ROWS - 1, :], ns_recv, pl.ds(0, k))]
    sources.append((m_rows.at[:, 0, :], m_rows.at[:, ROWS - 1, :], mask_recv, pl.ds(0, k)))
    for g in groups:
        span = spans[g]
        into = pl.ds(k + g * per * k, per * k)
        sources.append((t_rows.at[span, 0, :], t_rows.at[span, ROWS - 1, :], ns_recv, into))
    pl.semaphore_wait(barrier, jnp.where(has_south, 4, 3))
    rows_one = [row_copies(0, i, *source) for i, source in enumerate(sources)]
    for pair in rows_one[:3]:
        start_rows(pair)
    for load in loads[:4]:
        load.wait()
    m[...] = mi[...].astype(jnp.float32)
    pack_columns([(t, f * cells) for f in range(nt)] + [(u, 0), (m, 0)], ew_send)
    columns_one = column_copies(0, 0, ew_send, ew_recv)
    for copy in columns_one:
        copy.start()
    for pair in rows_one[3:]:
        start_rows(pair)
    for load in loads[4:]:
        load.wait()

    bottom = b[...]

    def inner_one(level, carry):
        lower, ratio = carry
        uu, vv, mm = tile(u, level), tile(v, level), tile(m, level)
        speed = 0.5 * (pltpu.roll(uu, 1, 1) + uu)
        is_open = jnp.where(lane == 0, 0.0, mm * pltpu.roll(mm, 1, 1))
        ahead = is_open * (jnp.maximum(speed, 0.0) + lateral_mixing)
        back = is_open * (lateral_mixing - jnp.minimum(speed, 0.0))
        c_west = ahead
        c_east = pltpu.roll(back, COLS - 1, 1)
        c_mid = -(back + pltpu.roll(ahead, COLS - 1, 1))
        speed = 0.5 * (pltpu.roll(vv, 1, 0) + vv)
        is_open = jnp.where(row == 0, 0.0, mm * pltpu.roll(mm, 1, 0))
        ahead = is_open * (jnp.maximum(speed, 0.0) + lateral_mixing)
        back = is_open * (lateral_mixing - jnp.minimum(speed, 0.0))
        c_south = ahead
        c_north = pltpu.roll(back, ROWS - 1, 0)
        c_mid = c_mid - (back + pltpu.roll(ahead, ROWS - 1, 0))
        for i, c in enumerate((c_west, c_east, c_south, c_north, c_mid)):
            put(coef, level, c, i)
        for f in range(nt):
            tt = tile(t, level, f)
            put(s1, level, tt + stencil(tt, c_west, c_east, c_south, c_north, c_mid), f)
        upper = jnp.where(level + 1 < bottom, tile(mix, level), 0.0)
        inverse = 1.0 / (1.0 + lower + upper + lower * ratio)
        ratio = -upper * inverse
        put(solve, level, inverse, 0)
        put(solve, level, ratio, 1)
        put(solve, level, lower * inverse, 2)
        return upper, ratio

    def stencil(tt, c_west, c_east, c_south, c_north, c_mid):
        return (
            (c_west * pltpu.roll(tt, 1, 1) + c_east * pltpu.roll(tt, COLS - 1, 1))
            + (c_south * pltpu.roll(tt, 1, 0) + c_north * pltpu.roll(tt, ROWS - 1, 0))
        ) + c_mid * tt

    zero = jnp.zeros((ROWS, COLS), jnp.float32)
    over_levels(k, inner_one, (zero, zero), 4)

    for copy in columns_one:
        copy.wait_recv()
    unpack_columns(ew_recv, y)

    def line(which, level, f):
        return ns_recv[which, pl.ds((1 + f) * k + level, 1), :]

    def wet(which, level):
        return wide_mask[which, pl.ds(level, 1), :]

    def outer_faces(level, carry):
        uu, vv, mm = tile(u, level), tile(v, level), tile(m, level)
        speed = 0.5 * (side(y, level, nt) + uu)
        is_open = jnp.where(ends, mm * side(y, level, nt + 1), 0.0)
        ahead = is_open * (jnp.maximum(speed, 0.0) + lateral_mixing)
        back = is_open * (lateral_mixing - jnp.minimum(speed, 0.0))
        c_side = jnp.where(lane < COLS // 2, ahead, back)
        c_more = -jnp.where(lane < COLS // 2, back, ahead)
        speed = 0.5 * (line(0, level, -1) + vv)
        is_open = jnp.where(row == 0, mm * wet(0, level), 0.0)
        c_south = is_open * (jnp.maximum(speed, 0.0) + lateral_mixing)
        c_more = c_more - is_open * (lateral_mixing - jnp.minimum(speed, 0.0))
        speed = 0.5 * (line(1, level, -1) + vv)
        is_open = jnp.where(row == ROWS - 1, mm * wet(1, level), 0.0)
        c_north = is_open * (lateral_mixing - jnp.minimum(speed, 0.0))
        c_more = c_more - is_open * (jnp.maximum(speed, 0.0) + lateral_mixing)
        for i, c in enumerate((c_side, c_south, c_north, c_more)):
            put(edge, level, c, i)
        put(coef, level, tile(coef, level, 4) + c_more, 4)
        return carry

    rows_two, columns_two, leaving = [], [], []
    for g in groups:
        mine = range(g * per, (g + 1) * per)

        def outer_one(level, carry):
            c_side, c_south, c_north, c_more = (tile(edge, level, i) for i in range(4))
            for f in mine:
                added = (c_side * side(y, level, f) + c_more * tile(t, level, f)) + (
                    c_south * line(0, level, f) + c_north * line(1, level, f)
                )
                put(s1, level, tile(s1, level, f) + added, f)
            return carry

        def inner_two(level, carry):
            c = [tile(coef, level, i) for i in range(5)]
            for f in mine:
                ss = tile(s1, level, f)
                put(rhs, level, 0.5 * ((tile(t, level, f) + ss) + stencil(ss, *c)), f)
            return carry

        if g == 0:
            rows_arrive(0, 0, *sources[0])
            rows_arrive(0, 1, *sources[1])
            wide_mask[...] = mask_recv[...].astype(jnp.float32)
            fold_rows(ns_recv, 0, k, flip=True)
            fold_rows(wide_mask, 0, k)
            over_levels(k, outer_faces, 0, k)
        rows_arrive(0, 2 + g, *sources[2 + g])
        fold_rows(ns_recv, k + g * per * k, per * k)
        over_levels(k, outer_one, 0, k)
        fields = [(s1, f * cells) for f in mine]
        pack_rows(fields, ns_send2, g * per * k)
        leaving.append((ns_send2.at[0, spans[g]], ns_send2.at[1, spans[g]], ns_recv2, spans[g]))
        rows_two.append(row_copies(1, g, *leaving[g]))
        start_rows(rows_two[g])
        pack_columns(fields, ew_send2.at[g])
        columns_two.append(column_copies(1, g, ew_send2.at[g], ew_recv2.at[g]))
        for copy in columns_two[g]:
            copy.start()
        over_levels(k, inner_two, 0, 8)

    for g in groups:
        mine = range(g * per, (g + 1) * per)
        sides = y2.at[g]

        def forward(level, carry):
            c_side, c_south, c_north = (0.5 * tile(edge, level, i) for i in range(3))
            inverse, carried = tile(solve, level, 0), tile(solve, level, 2)
            now = []
            for i, f in enumerate(mine):
                south = ns_recv2[0, pl.ds(f * k + level, 1), :]
                north = ns_recv2[1, pl.ds(f * k + level, 1), :]
                added = c_side * side(sides, level, i) + (c_south * south + c_north * north)
                value = (tile(rhs, level, f) + added) * inverse + carried * carry[i]
                put(rhs, level, value, f)
                now.append(value)
            return tuple(now)

        def backward(level, carry):
            ratio = tile(solve, level, 1)
            now = []
            for i, f in enumerate(mine):
                value = tile(rhs, level, f) - ratio * carry[i]
                put(out, level, value, f)
                now.append(value)
            return tuple(now)

        for copy in columns_two[g]:
            copy.wait_recv()
        unpack_columns(ew_recv2.at[g], sides)
        rows_arrive(1, g, *leaving[g])
        fold_rows(ns_recv2, g * per * k, per * k)
        over_levels(k, forward, (zero,) * per, k)
        over_levels(k, backward, (zero,) * per, k, backward=True)

    for pair in rows_one:
        pair[0].wait_send()
    for copy in columns_one:
        copy.wait_send()
    for g in groups:
        rows_two[g][0].wait_send()
        for copy in columns_two[g]:
            copy.wait_send()

    @pl.when(has_south)
    def _():
        for pair in rows_one + rows_two:
            pair[1].wait_send()


def on_device(n_lat, n_lon, tracer, east_vel, north_vel, wet_mask, bottom_level, vertical_mix):
    nt, k, rows, cols = tracer.shape
    cells = k * rows
    f32 = jnp.float32
    blocks = (nt + 2) * k * 2 // cols

    def vmem(*shape, dtype=f32):
        return pltpu.VMEM(shape, dtype)

    result = pl.pallas_call(
        functools.partial(kernel, nt, k, n_lat, n_lon),
        out_shape=pltpu.VMEM((nt * cells, cols), f32),
        in_specs=[pl.BlockSpec(memory_space=pltpu.HBM)] * 9,
        out_specs=pl.BlockSpec(memory_space=pltpu.VMEM),
        scratch_shapes=[
            vmem(nt * cells, cols),
            vmem(cells, cols),
            vmem(cells, cols),
            vmem(cells, cols, dtype=jnp.int32),
            vmem(rows, cols, dtype=jnp.int32),
            vmem(cells, cols),
            vmem(cells, cols),
            vmem(nt * cells, cols),
            vmem(nt * cells, cols),
            vmem(blocks, rows, cols),
            vmem(GROUPS, 1, rows, cols),
            vmem(5 * cells, cols),
            vmem(4 * cells, cols),
            vmem(3 * cells, cols),
            vmem(2, (nt + 1) * k, cols),
            vmem(2, k, cols, dtype=jnp.int32),
            vmem(2, k, cols),
            vmem(blocks, rows, cols),
            vmem(2, blocks, rows, cols),
            vmem(2, nt * k, cols),
            vmem(2, nt * k, cols),
            vmem(GROUPS, 1, rows, cols),
            vmem(GROUPS, 2, 1, rows, cols),
            pltpu.SemaphoreType.DMA((6,)),
            pltpu.SemaphoreType.DMA((2, GROUPS + 2, 4)),
            pltpu.SemaphoreType.DMA((2, GROUPS + 2, 4)),
        ],
        compiler_params=pltpu.CompilerParams(
            collective_id=0, has_side_effects=True, vmem_limit_bytes=62 * 1024 * 1024
        ),
    )(
        tracer.reshape(nt * cells, cols),
        east_vel.reshape(cells, cols),
        north_vel.reshape(cells, cols),
        wet_mask.reshape(cells, cols),
        bottom_level,
        vertical_mix.reshape(cells, cols),
        tracer.reshape(nt * k, rows, cols),
        north_vel,
        wet_mask,
    )
    return result.reshape(tracer.shape)


def solution(mesh):
    in_specs = (
        P(None, None, "lat", "lon"),
        P(None, "lat", "lon"),
        P(None, "lat", "lon"),
        P(None, "lat", "lon"),
        P("lat", "lon"),
        P(None, "lat", "lon"),
    )
    out_specs = P(None, None, "lat", "lon")
    return jax.shard_map(
        functools.partial(on_device, mesh.shape["lat"], mesh.shape["lon"]),
        mesh=mesh, in_specs=in_specs, out_specs=out_specs, check_vma=False,
    )
```

```python
import functools

import jax
import jax.numpy as jnp
from jax import lax
from jax.experimental import pallas as pl
from jax.experimental.pallas import tpu as pltpu
from jax.sharding import PartitionSpec as P

lateral_mixing = 0.08
MESH = pl.DeviceIdType.MESH
ROWS, COLS = 8, 128
GROUPS = 3


def over_levels(count, body, carry, unroll, backward=False):
    def some(step, carry):
        for part in range(unroll):
            level = step * unroll + part
            carry = body(count - 1 - level if backward else level, carry)
        return carry

    if unroll == count:
        return some(0, carry)
    return lax.fori_loop(0, count // unroll, some, carry)


def kernel(
    nt, k, n_lat, n_lon,
    t_hbm, u_hbm, v_hbm, m_hbm, b_hbm, mix_hbm, out,
    t, u, v, mi, b, mix, m, s1, rhs, y, y2, coef, edge, solve,
    ns_send, ns_recv, ew_send, ew_recv, ns_send2, ns_recv2, ew_send2, ew_recv2,
    load_sem, send_sem, recv_sem,
):
    lat, lon = lax.axis_index("lat"), lax.axis_index("lon")
    is_top = lat == n_lat - 1
    has_south = lat > 0
    east = lax.rem(lon + 1, n_lon)
    west = lax.rem(lon + n_lon - 1, n_lon)
    north_id = (jnp.where(is_top, lat, lat + 1), jnp.where(is_top, n_lon - 1 - lon, lon))
    south_id = (jnp.where(has_south, lat - 1, lat), lon)
    top_flag = jnp.where(is_top, 1, 0)
    cells = k * ROWS

    barrier = pltpu.get_barrier_semaphore()
    for target in ((lat, east), (lat, west), north_id):
        pl.semaphore_signal(barrier, inc=1, device_id=target, device_id_type=MESH)

    @pl.when(has_south)
    def _():
        pl.semaphore_signal(barrier, inc=1, device_id=south_id, device_id_type=MESH)

    per = nt // GROUPS
    groups = range(GROUPS)
    spans_one = [pl.ds(0, (2 + per) * k)] + [pl.ds((2 + g * per) * k, per * k) for g in groups[1:]]
    spans_two = [pl.ds(g * per * k, per * k) for g in groups]

    shares = [pl.ds(g * per * cells, per * cells) for g in groups]
    pairs = [(m_hbm, mi), (v_hbm, v)] + [(t_hbm.at[share], t.at[share]) for share in shares]
    pairs += [(u_hbm, u), (b_hbm, b), (mix_hbm, mix)]
    loads = [
        pltpu.make_async_copy(src, dst, load_sem.at[i]) for i, (src, dst) in enumerate(pairs)
    ]
    for load in loads:
        load.start()

    @pl.when(jnp.logical_not(has_south))
    def _():
        ns_recv[0] = jnp.zeros_like(ns_recv[0])
        ns_recv2[0] = jnp.zeros_like(ns_recv2[0])

    lane = lax.broadcasted_iota(jnp.int32, (ROWS, COLS), 1)
    row = lax.broadcasted_iota(jnp.int32, (ROWS, COLS), 0)
    ends = (lane == 0) | (lane == COLS - 1)

    def pack_rows(fields, send, start):
        for which, at in ((0, 0), (1, ROWS - 1)):
            for f, (ref, base) in enumerate(fields):
                send[which, pl.ds(start + f * k, k), :] = ref[pl.ds(base + at, k, stride=ROWS), :]

    def mirror_rows(send, span, flip):
        @pl.when(is_top)
        def _():
            a = lax.broadcasted_iota(jnp.int32, (COLS, COLS), 0)
            c = lax.broadcasted_iota(jnp.int32, (COLS, COLS), 1)
            mirror = jnp.where(a + c == COLS - 1, 1.0, 0.0).astype(jnp.bfloat16)
            rest = send[1, span, :]
            turned = None
            for _ in range(3):
                piece = rest.astype(jnp.bfloat16)
                rest = rest - piece.astype(jnp.float32)
                part = jnp.dot(piece, mirror, preferred_element_type=jnp.float32)
                turned = part if turned is None else turned + part
            send[1, span, :] = turned
            if flip:
                send[1, pl.ds(0, k), :] = -send[1, pl.ds(0, k), :]

    each = COLS // (2 * k)

    def pack_columns(fields, send):
        for block in range(send.shape[0]):
            packed = None
            for f, (ref, base) in enumerate(fields[block * each : (block + 1) * each]):
                for level in range(k):
                    at = 2 * (f * k + level)
                    moved = pltpu.roll(ref[pl.ds(base + level * ROWS, ROWS), :], at + 1, 1)
                    packed = moved if at == 0 else jnp.where(lane >= at, moved, packed)
            send[block] = packed

    def unpack_columns(recv, into):
        for block in range(recv.shape[1]):
            into[block] = jnp.where(
                lax.rem(lane, 2) == 0,
                pltpu.roll(recv[1, block], COLS - 1, 1),
                pltpu.roll(recv[0, block], 1, 1),
            )

    def side(ref, level, f):
        return pltpu.roll(ref[f // each], COLS - 1 - 2 * (f % each * k + level), 1)

    def remote(src, dst, phase, group, way, land, target):
        return pltpu.make_async_remote_copy(
            src_ref=src, dst_ref=dst, send_sem=send_sem.at[phase, group, way],
            recv_sem=recv_sem.at[phase, group, land], device_id=target, device_id_type=MESH,
        )

    def row_copies(phase, group, send, recv, span):
        north = remote(send.at[1, span], recv.at[top_flag, span], phase, group, 1, top_flag, north_id)
        south = remote(send.at[0, span], recv.at[1, span], phase, group, 0, 1, south_id)
        return north, south

    def column_copies(phase, group, send, recv):
        to_west = remote(send, recv.at[1], phase, group, 2, 2, (lat, west))
        to_east = remote(send, recv.at[0], phase, group, 3, 3, (lat, east))
        return to_west, to_east

    def start_rows(pair, send, span, flip):
        @pl.when(has_south)
        def _():
            pair[1].start()

        mirror_rows(send, span, flip)
        pair[0].start()

    def rows_arrive(phase, group, send, recv, span):
        remote(send.at[1, span], recv.at[1, span], phase, group, 1, 1, north_id).wait_recv()

        @pl.when(has_south)
        def _():
            remote(send.at[0, span], recv.at[0, span], phase, group, 0, 0, south_id).wait_recv()

    def place(level, f=0):
        if isinstance(level, int):
            return pl.ds(f * cells + level * ROWS, ROWS)
        return pl.ds(pl.multiple_of(f * cells + level * ROWS, ROWS), ROWS)

    def tile(ref, level, f=0):
        return ref[place(level, f), :]

    def put(ref, level, value, f=0):
        ref[place(level, f), :] = value

    for load in loads[:2]:
        load.wait()
    m[...] = mi[...].astype(jnp.float32)
    rows_one = []
    for g in groups:
        fields = [(t, f * cells) for f in range(g * per, (g + 1) * per)]
        if g == 0:
            fields = [(v, 0), (m, 0)] + fields
        loads[2 + g].wait()
        pack_rows(fields, ns_send, spans_one[g].start)
        if g == 0:
            pl.semaphore_wait(barrier, jnp.where(has_south, 4, 3))
        rows_one.append(row_copies(0, g, ns_send, ns_recv, spans_one[g]))
        start_rows(rows_one[g], ns_send, spans_one[g], g == 0)
        if g == GROUPS - 1:
            loads[2 + GROUPS].wait()
            pack_columns([(t, f * cells) for f in range(nt)] + [(u, 0), (m, 0)], ew_send)
            columns_one = column_copies(0, 0, ew_send, ew_recv)
            for copy in columns_one:
                copy.start()
    for load in loads[3 + GROUPS :]:
        load.wait()

    bottom = b[...]

    def inner_one(level, carry):
        lower, ratio = carry
        uu, vv, mm = tile(u, level), tile(v, level), tile(m, level)
        speed = 0.5 * (pltpu.roll(uu, 1, 1) + uu)
        is_open = jnp.where(lane == 0, 0.0, mm * pltpu.roll(mm, 1, 1))
        ahead = is_open * (jnp.maximum(speed, 0.0) + lateral_mixing)
        back = is_open * (lateral_mixing - jnp.minimum(speed, 0.0))
        c_west = ahead
        c_east = pltpu.roll(back, COLS - 1, 1)
        c_mid = -(back + pltpu.roll(ahead, COLS - 1, 1))
        speed = 0.5 * (pltpu.roll(vv, 1, 0) + vv)
        is_open = jnp.where(row == 0, 0.0, mm * pltpu.roll(mm, 1, 0))
        ahead = is_open * (jnp.maximum(speed, 0.0) + lateral_mixing)
        back = is_open * (lateral_mixing - jnp.minimum(speed, 0.0))
        c_south = ahead
        c_north = pltpu.roll(back, ROWS - 1, 0)
        c_mid = c_mid - (back + pltpu.roll(ahead, ROWS - 1, 0))
        for i, c in enumerate((c_west, c_east, c_south, c_north, c_mid)):
            put(coef, level, c, i)
        for f in range(nt):
            tt = tile(t, level, f)
            put(s1, level, tt + stencil(tt, c_west, c_east, c_south, c_north, c_mid), f)
        upper = jnp.where(level + 1 < bottom, tile(mix, level), 0.0)
        inverse = 1.0 / (1.0 + lower + upper + lower * ratio)
        ratio = -upper * inverse
        put(solve, level, inverse, 0)
        put(solve, level, ratio, 1)
        put(solve, level, lower * inverse, 2)
        return upper, ratio

    def stencil(tt, c_west, c_east, c_south, c_north, c_mid):
        return (
            (c_west * pltpu.roll(tt, 1, 1) + c_east * pltpu.roll(tt, COLS - 1, 1))
            + (c_south * pltpu.roll(tt, 1, 0) + c_north * pltpu.roll(tt, ROWS - 1, 0))
        ) + c_mid * tt

    zero = jnp.zeros((ROWS, COLS), jnp.float32)
    over_levels(k, inner_one, (zero, zero), 4)

    for copy in columns_one:
        copy.wait_recv()
    unpack_columns(ew_recv, y)

    def line(which, level, f):
        return ns_recv[which, pl.ds((2 + f) * k + level, 1), :]

    def outer_faces(level, carry):
        uu, vv, mm = tile(u, level), tile(v, level), tile(m, level)
        speed = 0.5 * (side(y, level, nt) + uu)
        is_open = jnp.where(ends, mm * side(y, level, nt + 1), 0.0)
        ahead = is_open * (jnp.maximum(speed, 0.0) + lateral_mixing)
        back = is_open * (lateral_mixing - jnp.minimum(speed, 0.0))
        c_side = jnp.where(lane < COLS // 2, ahead, back)
        c_more = -jnp.where(lane < COLS // 2, back, ahead)
        speed = 0.5 * (line(0, level, -2) + vv)
        is_open = jnp.where(row == 0, mm * line(0, level, -1), 0.0)
        c_south = is_open * (jnp.maximum(speed, 0.0) + lateral_mixing)
        c_more = c_more - is_open * (lateral_mixing - jnp.minimum(speed, 0.0))
        speed = 0.5 * (line(1, level, -2) + vv)
        is_open = jnp.where(row == ROWS - 1, mm * line(1, level, -1), 0.0)
        c_north = is_open * (lateral_mixing - jnp.minimum(speed, 0.0))
        c_more = c_more - is_open * (jnp.maximum(speed, 0.0) + lateral_mixing)
        for i, c in enumerate((c_side, c_south, c_north, c_more)):
            put(edge, level, c, i)
        put(coef, level, tile(coef, level, 4) + c_more, 4)
        return carry

    rows_two, columns_two = [], []
    for g in groups:
        mine = range(g * per, (g + 1) * per)

        def outer_one(level, carry):
            c_side, c_south, c_north, c_more = (tile(edge, level, i) for i in range(4))
            for f in mine:
                added = (c_side * side(y, level, f) + c_more * tile(t, level, f)) + (
                    c_south * line(0, level, f) + c_north * line(1, level, f)
                )
                put(s1, level, tile(s1, level, f) + added, f)
            return carry

        def inner_two(level, carry):
            c = [tile(coef, level, i) for i in range(5)]
            for f in mine:
                ss = tile(s1, level, f)
                put(rhs, level, 0.5 * ((tile(t, level, f) + ss) + stencil(ss, *c)), f)
            return carry

        rows_arrive(0, g, ns_send, ns_recv, spans_one[g])
        if g == 0:
            over_levels(k, outer_faces, 0, k)
        over_levels(k, outer_one, 0, k)
        fields = [(s1, f * cells) for f in mine]
        pack_rows(fields, ns_send2, g * per * k)
        rows_two.append(row_copies(1, g, ns_send2, ns_recv2, spans_two[g]))
        start_rows(rows_two[g], ns_send2, spans_two[g], False)
        pack_columns(fields, ew_send2.at[g])
        columns_two.append(column_copies(1, g, ew_send2.at[g], ew_recv2.at[g]))
        for copy in columns_two[g]:
            copy.start()
        over_levels(k, inner_two, 0, 8)

    for g in groups:
        mine = range(g * per, (g + 1) * per)
        sides = y2.at[g]

        def forward(level, carry):
            c_side, c_south, c_north = (0.5 * tile(edge, level, i) for i in range(3))
            inverse, carried = tile(solve, level, 0), tile(solve, level, 2)
            now = []
            for i, f in enumerate(mine):
                south = ns_recv2[0, pl.ds(f * k + level, 1), :]
                north = ns_recv2[1, pl.ds(f * k + level, 1), :]
                added = c_side * side(sides, level, i) + (c_south * south + c_north * north)
                value = (tile(rhs, level, f) + added) * inverse + carried * carry[i]
                put(rhs, level, value, f)
                now.append(value)
            return tuple(now)

        def backward(level, carry):
            ratio = tile(solve, level, 1)
            now = []
            for i, f in enumerate(mine):
                value = tile(rhs, level, f) - ratio * carry[i]
                put(out, level, value, f)
                now.append(value)
            return tuple(now)

        for copy in columns_two[g]:
            copy.wait_recv()
        unpack_columns(ew_recv2.at[g], sides)
        rows_arrive(1, g, ns_send2, ns_recv2, spans_two[g])
        over_levels(k, forward, (zero,) * per, k)
        over_levels(k, backward, (zero,) * per, k, backward=True)

    for copy in columns_one:
        copy.wait_send()
    for g in groups:
        rows_one[g][0].wait_send()
        rows_two[g][0].wait_send()
        for copy in columns_two[g]:
            copy.wait_send()

    @pl.when(has_south)
    def _():
        for pair in rows_one + rows_two:
            pair[1].wait_send()


def on_device(n_lat, n_lon, tracer, east_vel, north_vel, wet_mask, bottom_level, vertical_mix):
    nt, k, rows, cols = tracer.shape
    cells = k * rows
    f32 = jnp.float32
    blocks = (nt + 2) * k * 2 // cols

    def vmem(*shape, dtype=f32):
        return pltpu.VMEM(shape, dtype)

    result = pl.pallas_call(
        functools.partial(kernel, nt, k, n_lat, n_lon),
        out_shape=pltpu.VMEM((nt * cells, cols), f32),
        in_specs=[pl.BlockSpec(memory_space=pltpu.HBM)] * 6,
        out_specs=pl.BlockSpec(memory_space=pltpu.VMEM),
        scratch_shapes=[
            vmem(nt * cells, cols),
            vmem(cells, cols),
            vmem(cells, cols),
            vmem(cells, cols, dtype=jnp.int32),
            vmem(rows, cols, dtype=jnp.int32),
            vmem(cells, cols),
            vmem(cells, cols),
            vmem(nt * cells, cols),
            vmem(nt * cells, cols),
            vmem(blocks, rows, cols),
            vmem(GROUPS, 1, rows, cols),
            vmem(5 * cells, cols),
            vmem(4 * cells, cols),
            vmem(3 * cells, cols),
            vmem(2, (nt + 2) * k, cols),
            vmem(2, (nt + 2) * k, cols),
            vmem(blocks, rows, cols),
            vmem(2, blocks, rows, cols),
            vmem(2, nt * k, cols),
            vmem(2, nt * k, cols),
            vmem(GROUPS, 1, rows, cols),
            vmem(GROUPS, 2, 1, rows, cols),
            pltpu.SemaphoreType.DMA((5 + GROUPS,)),
            pltpu.SemaphoreType.DMA((2, GROUPS, 4)),
            pltpu.SemaphoreType.DMA((2, GROUPS, 4)),
        ],
        compiler_params=pltpu.CompilerParams(
            collective_id=0, has_side_effects=True, vmem_limit_bytes=62 * 1024 * 1024
        ),
    )(
        tracer.reshape(nt * cells, cols),
        east_vel.reshape(cells, cols),
        north_vel.reshape(cells, cols),
        wet_mask.reshape(cells, cols),
        bottom_level,
        vertical_mix.reshape(cells, cols),
    )
    return result.reshape(tracer.shape)


def solution(mesh):
    in_specs = (
        P(None, None, "lat", "lon"),
        P(None, "lat", "lon"),
        P(None, "lat", "lon"),
        P(None, "lat", "lon"),
        P("lat", "lon"),
        P(None, "lat", "lon"),
    )
    out_specs = P(None, None, "lat", "lon")
    return jax.shard_map(
        functools.partial(on_device, mesh.shape["lat"], mesh.shape["lon"]),
        mesh=mesh, in_specs=in_specs, out_specs=out_specs, check_vma=False,
    )
```

```python
import functools

import jax
import jax.numpy as jnp
from jax import lax
from jax.experimental import pallas as pl
from jax.experimental.pallas import tpu as pltpu
from jax.sharding import PartitionSpec as P

lateral_mixing = 0.08
MESH = pl.DeviceIdType.MESH
ROWS, COLS = 8, 128
GROUPS = 3


def over_levels(count, body, carry, unroll, backward=False):
    def some(step, carry):
        for part in range(unroll):
            level = step * unroll + part
            carry = body(count - 1 - level if backward else level, carry)
        return carry

    if unroll == count:
        return some(0, carry)
    return lax.fori_loop(0, count // unroll, some, carry)


def kernel(
    nt, k, n_lat, n_lon,
    t_hbm, u_hbm, v_hbm, m_hbm, b_hbm, mix_hbm, out,
    t, u, v, mi, b, mix, m, s1, rhs, y, y2, coef, edge, solve,
    ns_send, ns_recv, ew_send, ew_recv, ns_send2, ns_recv2, ew_send2, ew_recv2,
    load_sem, send_sem, recv_sem,
):
    lat, lon = lax.axis_index("lat"), lax.axis_index("lon")
    is_top = lat == n_lat - 1
    has_south = lat > 0
    east = lax.rem(lon + 1, n_lon)
    west = lax.rem(lon + n_lon - 1, n_lon)
    north_id = (jnp.where(is_top, lat, lat + 1), jnp.where(is_top, n_lon - 1 - lon, lon))
    south_id = (jnp.where(has_south, lat - 1, lat), lon)
    top_flag = jnp.where(is_top, 1, 0)
    cells = k * ROWS

    barrier = pltpu.get_barrier_semaphore()
    for target in ((lat, east), (lat, west), north_id):
        pl.semaphore_signal(barrier, inc=1, device_id=target, device_id_type=MESH)

    @pl.when(has_south)
    def _():
        pl.semaphore_signal(barrier, inc=1, device_id=south_id, device_id_type=MESH)

    per = nt // GROUPS
    groups = range(GROUPS)
    spans_one = [pl.ds(0, (2 + per) * k)] + [pl.ds((2 + g * per) * k, per * k) for g in groups[1:]]
    spans_two = [pl.ds(g * per * k, per * k) for g in groups]

    shares = [pl.ds(g * per * cells, per * cells) for g in groups]
    pairs = [(m_hbm, mi), (v_hbm, v)] + [(t_hbm.at[share], t.at[share]) for share in shares]
    pairs += [(u_hbm, u), (b_hbm, b), (mix_hbm, mix)]
    loads = [
        pltpu.make_async_copy(src, dst, load_sem.at[i]) for i, (src, dst) in enumerate(pairs)
    ]
    for load in loads:
        load.start()

    @pl.when(jnp.logical_not(has_south))
    def _():
        ns_recv[0] = jnp.zeros_like(ns_recv[0])
        ns_recv2[0] = jnp.zeros_like(ns_recv2[0])

    lane = lax.broadcasted_iota(jnp.int32, (ROWS, COLS), 1)
    row = lax.broadcasted_iota(jnp.int32, (ROWS, COLS), 0)
    ends = (lane == 0) | (lane == COLS - 1)

    def pack_rows(fields, send, start):
        for which, at in ((0, 0), (1, ROWS - 1)):
            for f, (ref, base) in enumerate(fields):
                send[which, pl.ds(start + f * k, k), :] = ref[pl.ds(base + at, k, stride=ROWS), :]

    def mirror_rows(send, span, flip):
        @pl.when(is_top)
        def _():
            a = lax.broadcasted_iota(jnp.int32, (COLS, COLS), 0)
            c = lax.broadcasted_iota(jnp.int32, (COLS, COLS), 1)
            mirror = jnp.where(a + c == COLS - 1, 1.0, 0.0).astype(jnp.bfloat16)
            rest = send[1, span, :]
            turned = None
            for _ in range(3):
                piece = rest.astype(jnp.bfloat16)
                rest = rest - piece.astype(jnp.float32)
                part = jnp.dot(piece, mirror, preferred_element_type=jnp.float32)
                turned = part if turned is None else turned + part
            send[1, span, :] = turned
            if flip:
                send[1, pl.ds(0, k), :] = -send[1, pl.ds(0, k), :]

    each = COLS // (2 * k)

    def pack_columns(fields, send):
        for block in range(send.shape[0]):
            packed = None
            for f, (ref, base) in enumerate(fields[block * each : (block + 1) * each]):
                for level in range(k):
                    at = 2 * (f * k + level)
                    moved = pltpu.roll(ref[pl.ds(base + level * ROWS, ROWS), :], at + 1, 1)
                    packed = moved if at == 0 else jnp.where(lane >= at, moved, packed)
            send[block] = packed

    def unpack_columns(recv, into):
        for block in range(recv.shape[1]):
            into[block] = jnp.where(
                lax.rem(lane, 2) == 0,
                pltpu.roll(recv[1, block], COLS - 1, 1),
                pltpu.roll(recv[0, block], 1, 1),
            )

    def side(ref, level, f):
        return pltpu.roll(ref[f // each], COLS - 1 - 2 * (f % each * k + level), 1)

    def remote(src, dst, phase, group, way, land, target):
        return pltpu.make_async_remote_copy(
            src_ref=src, dst_ref=dst, send_sem=send_sem.at[phase, group, way],
            recv_sem=recv_sem.at[phase, group, land], device_id=target, device_id_type=MESH,
        )

    def row_copies(phase, group, send, recv, span):
        north = remote(send.at[1, span], recv.at[top_flag, span], phase, group, 1, top_flag, north_id)
        south = remote(send.at[0, span], recv.at[1, span], phase, group, 0, 1, south_id)
        return north, south

    def column_copies(phase, group, send, recv):
        to_west = remote(send, recv.at[1], phase, group, 2, 2, (lat, west))
        to_east = remote(send, recv.at[0], phase, group, 3, 3, (lat, east))
        return to_west, to_east

    def start_rows(pair, send, span, flip):
        @pl.when(has_south)
        def _():
            pair[1].start()

        mirror_rows(send, span, flip)
        pair[0].start()

    def rows_arrive(phase, group, send, recv, span):
        remote(send.at[1, span], recv.at[1, span], phase, group, 1, 1, north_id).wait_recv()

        @pl.when(has_south)
        def _():
            remote(send.at[0, span], recv.at[0, span], phase, group, 0, 0, south_id).wait_recv()

    def place(level, f=0):
        if isinstance(level, int):
            return pl.ds(f * cells + level * ROWS, ROWS)
        return pl.ds(pl.multiple_of(f * cells + level * ROWS, ROWS), ROWS)

    def tile(ref, level, f=0):
        return ref[place(level, f), :]

    def put(ref, level, value, f=0):
        ref[place(level, f), :] = value

    for load in loads[:2]:
        load.wait()
    m[...] = mi[...].astype(jnp.float32)
    for load in loads[2 : 3 + GROUPS]:
        load.wait()
    pack_columns([(t, f * cells) for f in range(nt)] + [(u, 0), (m, 0)], ew_send)
    columns_one = column_copies(0, 0, ew_send, ew_recv)
    rows_one = []
    for g in groups:
        fields = [(t, f * cells) for f in range(g * per, (g + 1) * per)]
        if g == 0:
            fields = [(v, 0), (m, 0)] + fields
        pack_rows(fields, ns_send, spans_one[g].start)
        if g == 0:
            pl.semaphore_wait(barrier, jnp.where(has_south, 4, 3))
            for copy in columns_one:
                copy.start()
        rows_one.append(row_copies(0, g, ns_send, ns_recv, spans_one[g]))
        start_rows(rows_one[g], ns_send, spans_one[g], g == 0)
    for load in loads[3 + GROUPS :]:
        load.wait()

    bottom = b[...]

    def inner_one(level, carry):
        lower, ratio = carry
        uu, vv, mm = tile(u, level), tile(v, level), tile(m, level)
        speed = 0.5 * (pltpu.roll(uu, 1, 1) + uu)
        is_open = jnp.where(lane == 0, 0.0, mm * pltpu.roll(mm, 1, 1))
        ahead = is_open * (jnp.maximum(speed, 0.0) + lateral_mixing)
        back = is_open * (lateral_mixing - jnp.minimum(speed, 0.0))
        c_west = ahead
        c_east = pltpu.roll(back, COLS - 1, 1)
        c_mid = -(back + pltpu.roll(ahead, COLS - 1, 1))
        speed = 0.5 * (pltpu.roll(vv, 1, 0) + vv)
        is_open = jnp.where(row == 0, 0.0, mm * pltpu.roll(mm, 1, 0))
        ahead = is_open * (jnp.maximum(speed, 0.0) + lateral_mixing)
        back = is_open * (lateral_mixing - jnp.minimum(speed, 0.0))
        c_south = ahead
        c_north = pltpu.roll(back, ROWS - 1, 0)
        c_mid = c_mid - (back + pltpu.roll(ahead, ROWS - 1, 0))
        for i, c in enumerate((c_west, c_east, c_south, c_north, c_mid)):
            put(coef, level, c, i)
        for f in range(nt):
            tt = tile(t, level, f)
            put(s1, level, tt + stencil(tt, c_west, c_east, c_south, c_north, c_mid), f)
        upper = jnp.where(level + 1 < bottom, tile(mix, level), 0.0)
        inverse = 1.0 / (1.0 + lower + upper + lower * ratio)
        ratio = -upper * inverse
        put(solve, level, inverse, 0)
        put(solve, level, ratio, 1)
        put(solve, level, lower * inverse, 2)
        return upper, ratio

    def stencil(tt, c_west, c_east, c_south, c_north, c_mid):
        return (
            (c_west * pltpu.roll(tt, 1, 1) + c_east * pltpu.roll(tt, COLS - 1, 1))
            + (c_south * pltpu.roll(tt, 1, 0) + c_north * pltpu.roll(tt, ROWS - 1, 0))
        ) + c_mid * tt

    zero = jnp.zeros((ROWS, COLS), jnp.float32)
    over_levels(k, inner_one, (zero, zero), 4)

    for copy in columns_one:
        copy.wait_recv()
    unpack_columns(ew_recv, y)

    def line(which, level, f):
        return ns_recv[which, pl.ds((2 + f) * k + level, 1), :]

    def outer_faces(level, carry):
        uu, vv, mm = tile(u, level), tile(v, level), tile(m, level)
        speed = 0.5 * (side(y, level, nt) + uu)
        is_open = jnp.where(ends, mm * side(y, level, nt + 1), 0.0)
        ahead = is_open * (jnp.maximum(speed, 0.0) + lateral_mixing)
        back = is_open * (lateral_mixing - jnp.minimum(speed, 0.0))
        c_side = jnp.where(lane < COLS // 2, ahead, back)
        c_more = -jnp.where(lane < COLS // 2, back, ahead)
        speed = 0.5 * (line(0, level, -2) + vv)
        is_open = jnp.where(row == 0, mm * line(0, level, -1), 0.0)
        c_south = is_open * (jnp.maximum(speed, 0.0) + lateral_mixing)
        c_more = c_more - is_open * (lateral_mixing - jnp.minimum(speed, 0.0))
        speed = 0.5 * (line(1, level, -2) + vv)
        is_open = jnp.where(row == ROWS - 1, mm * line(1, level, -1), 0.0)
        c_north = is_open * (lateral_mixing - jnp.minimum(speed, 0.0))
        c_more = c_more - is_open * (jnp.maximum(speed, 0.0) + lateral_mixing)
        for i, c in enumerate((c_side, c_south, c_north, c_more)):
            put(edge, level, c, i)
        put(coef, level, tile(coef, level, 4) + c_more, 4)
        return carry

    rows_two, columns_two = [], []
    for g in groups:
        mine = range(g * per, (g + 1) * per)

        def outer_one(level, carry):
            c_side, c_south, c_north, c_more = (tile(edge, level, i) for i in range(4))
            for f in mine:
                added = (c_side * side(y, level, f) + c_more * tile(t, level, f)) + (
                    c_south * line(0, level, f) + c_north * line(1, level, f)
                )
                put(s1, level, tile(s1, level, f) + added, f)
            return carry

        def inner_two(level, carry):
            c = [tile(coef, level, i) for i in range(5)]
            for f in mine:
                ss = tile(s1, level, f)
                put(rhs, level, 0.5 * ((tile(t, level, f) + ss) + stencil(ss, *c)), f)
            return carry

        rows_arrive(0, g, ns_send, ns_recv, spans_one[g])
        if g == 0:
            over_levels(k, outer_faces, 0, k)
        over_levels(k, outer_one, 0, k)
        fields = [(s1, f * cells) for f in mine]
        pack_columns(fields, ew_send2.at[g])
        columns_two.append(column_copies(1, g, ew_send2.at[g], ew_recv2.at[g]))
        for copy in columns_two[g]:
            copy.start()
        pack_rows(fields, ns_send2, g * per * k)
        rows_two.append(row_copies(1, g, ns_send2, ns_recv2, spans_two[g]))
        start_rows(rows_two[g], ns_send2, spans_two[g], False)
        over_levels(k, inner_two, 0, 8)

    for g in groups:
        mine = range(g * per, (g + 1) * per)
        sides = y2.at[g]

        def forward(level, carry):
            c_side, c_south, c_north = (0.5 * tile(edge, level, i) for i in range(3))
            inverse, carried = tile(solve, level, 0), tile(solve, level, 2)
            now = []
            for i, f in enumerate(mine):
                south = ns_recv2[0, pl.ds(f * k + level, 1), :]
                north = ns_recv2[1, pl.ds(f * k + level, 1), :]
                added = c_side * side(sides, level, i) + (c_south * south + c_north * north)
                value = (tile(rhs, level, f) + added) * inverse + carried * carry[i]
                put(rhs, level, value, f)
                now.append(value)
            return tuple(now)

        def backward(level, carry):
            ratio = tile(solve, level, 1)
            now = []
            for i, f in enumerate(mine):
                value = tile(rhs, level, f) - ratio * carry[i]
                put(out, level, value, f)
                now.append(value)
            return tuple(now)

        for copy in columns_two[g]:
            copy.wait_recv()
        unpack_columns(ew_recv2.at[g], sides)
        rows_arrive(1, g, ns_send2, ns_recv2, spans_two[g])
        over_levels(k, forward, (zero,) * per, k)
        over_levels(k, backward, (zero,) * per, k, backward=True)

    for copy in columns_one:
        copy.wait_send()
    for g in groups:
        rows_one[g][0].wait_send()
        rows_two[g][0].wait_send()
        for copy in columns_two[g]:
            copy.wait_send()

    @pl.when(has_south)
    def _():
        for pair in rows_one + rows_two:
            pair[1].wait_send()


def on_device(n_lat, n_lon, tracer, east_vel, north_vel, wet_mask, bottom_level, vertical_mix):
    nt, k, rows, cols = tracer.shape
    cells = k * rows
    f32 = jnp.float32
    blocks = (nt + 2) * k * 2 // cols

    def vmem(*shape, dtype=f32):
        return pltpu.VMEM(shape, dtype)

    result = pl.pallas_call(
        functools.partial(kernel, nt, k, n_lat, n_lon),
        out_shape=pltpu.VMEM((nt * cells, cols), f32),
        in_specs=[pl.BlockSpec(memory_space=pltpu.HBM)] * 6,
        out_specs=pl.BlockSpec(memory_space=pltpu.VMEM),
        scratch_shapes=[
            vmem(nt * cells, cols),
            vmem(cells, cols),
            vmem(cells, cols),
            vmem(cells, cols, dtype=jnp.int32),
            vmem(rows, cols, dtype=jnp.int32),
            vmem(cells, cols),
            vmem(cells, cols),
            vmem(nt * cells, cols),
            vmem(nt * cells, cols),
            vmem(blocks, rows, cols),
            vmem(GROUPS, 1, rows, cols),
            vmem(5 * cells, cols),
            vmem(4 * cells, cols),
            vmem(3 * cells, cols),
            vmem(2, (nt + 2) * k, cols),
            vmem(2, (nt + 2) * k, cols),
            vmem(blocks, rows, cols),
            vmem(2, blocks, rows, cols),
            vmem(2, nt * k, cols),
            vmem(2, nt * k, cols),
            vmem(GROUPS, 1, rows, cols),
            vmem(GROUPS, 2, 1, rows, cols),
            pltpu.SemaphoreType.DMA((5 + GROUPS,)),
            pltpu.SemaphoreType.DMA((2, GROUPS, 4)),
            pltpu.SemaphoreType.DMA((2, GROUPS, 4)),
        ],
        compiler_params=pltpu.CompilerParams(
            collective_id=0, has_side_effects=True, vmem_limit_bytes=62 * 1024 * 1024
        ),
    )(
        tracer.reshape(nt * cells, cols),
        east_vel.reshape(cells, cols),
        north_vel.reshape(cells, cols),
        wet_mask.reshape(cells, cols),
        bottom_level,
        vertical_mix.reshape(cells, cols),
    )
    return result.reshape(tracer.shape)


def solution(mesh):
    in_specs = (
        P(None, None, "lat", "lon"),
        P(None, "lat", "lon"),
        P(None, "lat", "lon"),
        P(None, "lat", "lon"),
        P("lat", "lon"),
        P(None, "lat", "lon"),
    )
    out_specs = P(None, None, "lat", "lon")
    return jax.shard_map(
        functools.partial(on_device, mesh.shape["lat"], mesh.shape["lon"]),
        mesh=mesh, in_specs=in_specs, out_specs=out_specs, check_vma=False,
    )
```

```python
import functools

import jax
import jax.numpy as jnp
from jax import lax
from jax.experimental import pallas as pl
from jax.experimental.pallas import tpu as pltpu
from jax.sharding import PartitionSpec as P

lateral_mixing = 0.08
MESH = pl.DeviceIdType.MESH
ROWS, COLS = 8, 128
GROUPS = 3


def over_levels(count, body, carry, unroll, backward=False):
    def some(step, carry):
        for part in range(unroll):
            level = step * unroll + part
            carry = body(count - 1 - level if backward else level, carry)
        return carry

    if unroll == count:
        return some(0, carry)
    return lax.fori_loop(0, count // unroll, some, carry)


def kernel(
    nt, k, n_lat, n_lon,
    t_hbm, u_hbm, v_hbm, m_hbm, b_hbm, mix_hbm, out,
    t, u, v, mi, b, mix, m, s1, rhs, y, y2, coef, edge, solve,
    ns_send, ns_recv, ew_send, ew_recv, ns_send2, ns_recv2, ew_send2, ew_recv2,
    load_sem, send_sem, recv_sem,
):
    lat, lon = lax.axis_index("lat"), lax.axis_index("lon")
    is_top = lat == n_lat - 1
    has_south = lat > 0
    east = lax.rem(lon + 1, n_lon)
    west = lax.rem(lon + n_lon - 1, n_lon)
    north_id = (jnp.where(is_top, lat, lat + 1), jnp.where(is_top, n_lon - 1 - lon, lon))
    south_id = (jnp.where(has_south, lat - 1, lat), lon)
    top_flag = jnp.where(is_top, 1, 0)
    cells = k * ROWS

    barrier = pltpu.get_barrier_semaphore()
    for target in ((lat, east), (lat, west), north_id):
        pl.semaphore_signal(barrier, inc=1, device_id=target, device_id_type=MESH)

    @pl.when(has_south)
    def _():
        pl.semaphore_signal(barrier, inc=1, device_id=south_id, device_id_type=MESH)

    per = nt // GROUPS
    groups = range(GROUPS)
    spans_one = [pl.ds(0, (2 + per) * k)] + [pl.ds((2 + g * per) * k, per * k) for g in groups[1:]]
    spans_two = [pl.ds(g * per * k, per * k) for g in groups]

    shares = [pl.ds(g * per * cells, per * cells) for g in groups]
    pairs = [(m_hbm, mi), (v_hbm, v)] + [(t_hbm.at[share], t.at[share]) for share in shares]
    pairs += [(u_hbm, u), (b_hbm, b), (mix_hbm, mix)]
    loads = [
        pltpu.make_async_copy(src, dst, load_sem.at[i]) for i, (src, dst) in enumerate(pairs)
    ]
    for load in loads:
        load.start()

    @pl.when(jnp.logical_not(has_south))
    def _():
        ns_recv[0] = jnp.zeros_like(ns_recv[0])
        ns_recv2[0] = jnp.zeros_like(ns_recv2[0])

    lane = lax.broadcasted_iota(jnp.int32, (ROWS, COLS), 1)
    row = lax.broadcasted_iota(jnp.int32, (ROWS, COLS), 0)
    ends = (lane == 0) | (lane == COLS - 1)

    def pack_rows(fields, send, start):
        for which, at in ((0, 0), (1, ROWS - 1)):
            for f, (ref, base) in enumerate(fields):
                send[which, pl.ds(start + f * k, k), :] = ref[pl.ds(base + at, k, stride=ROWS), :]

    def mirror_rows(send, span, flip):
        @pl.when(is_top)
        def _():
            a = lax.broadcasted_iota(jnp.int32, (COLS, COLS), 0)
            c = lax.broadcasted_iota(jnp.int32, (COLS, COLS), 1)
            mirror = jnp.where(a + c == COLS - 1, 1.0, 0.0).astype(jnp.bfloat16)
            rest = send[1, span, :]
            turned = None
            for _ in range(3):
                piece = rest.astype(jnp.bfloat16)
                rest = rest - piece.astype(jnp.float32)
                part = jnp.dot(piece, mirror, preferred_element_type=jnp.float32)
                turned = part if turned is None else turned + part
            send[1, span, :] = turned
            if flip:
                send[1, pl.ds(0, k), :] = -send[1, pl.ds(0, k), :]

    each = COLS // (2 * k)

    def pack_columns(fields, send):
        for block in range(send.shape[0]):
            packed = None
            for f, (ref, base) in enumerate(fields[block * each : (block + 1) * each]):
                for level in range(k):
                    at = 2 * (f * k + level)
                    moved = pltpu.roll(ref[pl.ds(base + level * ROWS, ROWS), :], at + 1, 1)
                    packed = moved if at == 0 else jnp.where(lane >= at, moved, packed)
            send[block] = packed

    def unpack_columns(recv, into):
        for block in range(recv.shape[1]):
            into[block] = jnp.where(
                lax.rem(lane, 2) == 0,
                pltpu.roll(recv[1, block], COLS - 1, 1),
                pltpu.roll(recv[0, block], 1, 1),
            )

    def side(ref, level, f):
        return pltpu.roll(ref[f // each], COLS - 1 - 2 * (f % each * k + level), 1)

    def remote(src, dst, phase, group, way, land, target):
        return pltpu.make_async_remote_copy(
            src_ref=src, dst_ref=dst, send_sem=send_sem.at[phase, group, way],
            recv_sem=recv_sem.at[phase, group, land], device_id=target, device_id_type=MESH,
        )

    def row_copies(phase, group, send, recv, span):
        north = remote(send.at[1, span], recv.at[top_flag, span], phase, group, 1, top_flag, north_id)
        south = remote(send.at[0, span], recv.at[1, span], phase, group, 0, 1, south_id)
        return north, south

    def column_copies(phase, group, send, recv):
        to_west = remote(send, recv.at[1], phase, group, 2, 2, (lat, west))
        to_east = remote(send, recv.at[0], phase, group, 3, 3, (lat, east))
        return to_west, to_east

    def start_rows(pair):
        pair[0].start()

        @pl.when(has_south)
        def _():
            pair[1].start()

    def rows_arrive(phase, group, send, recv, span):
        remote(send.at[1, span], recv.at[1, span], phase, group, 1, 1, north_id).wait_recv()

        @pl.when(has_south)
        def _():
            remote(send.at[0, span], recv.at[0, span], phase, group, 0, 0, south_id).wait_recv()

    def place(level, f=0):
        if isinstance(level, int):
            return pl.ds(f * cells + level * ROWS, ROWS)
        return pl.ds(pl.multiple_of(f * cells + level * ROWS, ROWS), ROWS)

    def tile(ref, level, f=0):
        return ref[place(level, f), :]

    def put(ref, level, value, f=0):
        ref[place(level, f), :] = value

    for load in loads[:2]:
        load.wait()
    m[...] = mi[...].astype(jnp.float32)
    for load in loads[2 : 3 + GROUPS]:
        load.wait()
    pack_columns([(t, f * cells) for f in range(nt)] + [(u, 0), (m, 0)], ew_send)
    columns_one = column_copies(0, 0, ew_send, ew_recv)
    rows_one = []
    for g in groups:
        fields = [(t, f * cells) for f in range(g * per, (g + 1) * per)]
        if g == 0:
            fields = [(v, 0), (m, 0)] + fields
        pack_rows(fields, ns_send, spans_one[g].start)
        mirror_rows(ns_send, spans_one[g], g == 0)
        if g == 0:
            pl.semaphore_wait(barrier, jnp.where(has_south, 4, 3))
            for copy in columns_one:
                copy.start()
        rows_one.append(row_copies(0, g, ns_send, ns_recv, spans_one[g]))
        start_rows(rows_one[g])
    for load in loads[3 + GROUPS :]:
        load.wait()

    bottom = b[...]

    def inner_one(level, carry):
        lower, ratio = carry
        uu, vv, mm = tile(u, level), tile(v, level), tile(m, level)
        speed = 0.5 * (pltpu.roll(uu, 1, 1) + uu)
        is_open = jnp.where(lane == 0, 0.0, mm * pltpu.roll(mm, 1, 1))
        ahead = is_open * (jnp.maximum(speed, 0.0) + lateral_mixing)
        back = is_open * (lateral_mixing - jnp.minimum(speed, 0.0))
        c_west = ahead
        c_east = pltpu.roll(back, COLS - 1, 1)
        c_mid = -(back + pltpu.roll(ahead, COLS - 1, 1))
        speed = 0.5 * (pltpu.roll(vv, 1, 0) + vv)
        is_open = jnp.where(row == 0, 0.0, mm * pltpu.roll(mm, 1, 0))
        ahead = is_open * (jnp.maximum(speed, 0.0) + lateral_mixing)
        back = is_open * (lateral_mixing - jnp.minimum(speed, 0.0))
        c_south = ahead
        c_north = pltpu.roll(back, ROWS - 1, 0)
        c_mid = c_mid - (back + pltpu.roll(ahead, ROWS - 1, 0))
        for i, c in enumerate((c_west, c_east, c_south, c_north, c_mid)):
            put(coef, level, c, i)
        for f in range(nt):
            tt = tile(t, level, f)
            put(s1, level, tt + stencil(tt, c_west, c_east, c_south, c_north, c_mid), f)
        upper = jnp.where(level + 1 < bottom, tile(mix, level), 0.0)
        inverse = 1.0 / (1.0 + lower + upper + lower * ratio)
        ratio = -upper * inverse
        put(solve, level, inverse, 0)
        put(solve, level, ratio, 1)
        put(solve, level, lower * inverse, 2)
        return upper, ratio

    def stencil(tt, c_west, c_east, c_south, c_north, c_mid):
        return (
            (c_west * pltpu.roll(tt, 1, 1) + c_east * pltpu.roll(tt, COLS - 1, 1))
            + (c_south * pltpu.roll(tt, 1, 0) + c_north * pltpu.roll(tt, ROWS - 1, 0))
        ) + c_mid * tt

    zero = jnp.zeros((ROWS, COLS), jnp.float32)
    over_levels(k, inner_one, (zero, zero), 4)

    for copy in columns_one:
        copy.wait_recv()
    unpack_columns(ew_recv, y)

    def line(which, level, f):
        return ns_recv[which, pl.ds((2 + f) * k + level, 1), :]

    def outer_faces(level, carry):
        uu, vv, mm = tile(u, level), tile(v, level), tile(m, level)
        speed = 0.5 * (side(y, level, nt) + uu)
        is_open = jnp.where(ends, mm * side(y, level, nt + 1), 0.0)
        ahead = is_open * (jnp.maximum(speed, 0.0) + lateral_mixing)
        back = is_open * (lateral_mixing - jnp.minimum(speed, 0.0))
        c_side = jnp.where(lane < COLS // 2, ahead, back)
        c_more = -jnp.where(lane < COLS // 2, back, ahead)
        speed = 0.5 * (line(0, level, -2) + vv)
        is_open = jnp.where(row == 0, mm * line(0, level, -1), 0.0)
        c_south = is_open * (jnp.maximum(speed, 0.0) + lateral_mixing)
        c_more = c_more - is_open * (lateral_mixing - jnp.minimum(speed, 0.0))
        speed = 0.5 * (line(1, level, -2) + vv)
        is_open = jnp.where(row == ROWS - 1, mm * line(1, level, -1), 0.0)
        c_north = is_open * (lateral_mixing - jnp.minimum(speed, 0.0))
        c_more = c_more - is_open * (jnp.maximum(speed, 0.0) + lateral_mixing)
        for i, c in enumerate((c_side, c_south, c_north, c_more)):
            put(edge, level, c, i)
        put(coef, level, tile(coef, level, 4) + c_more, 4)
        return carry

    rows_two, columns_two = [], []
    for g in groups:
        mine = range(g * per, (g + 1) * per)

        def outer_one(level, carry):
            c_side, c_south, c_north, c_more = (tile(edge, level, i) for i in range(4))
            for f in mine:
                added = (c_side * side(y, level, f) + c_more * tile(t, level, f)) + (
                    c_south * line(0, level, f) + c_north * line(1, level, f)
                )
                put(s1, level, tile(s1, level, f) + added, f)
            return carry

        def inner_two(level, carry):
            c = [tile(coef, level, i) for i in range(5)]
            for f in mine:
                ss = tile(s1, level, f)
                put(rhs, level, 0.5 * ((tile(t, level, f) + ss) + stencil(ss, *c)), f)
            return carry

        rows_arrive(0, g, ns_send, ns_recv, spans_one[g])
        if g == 0:
            over_levels(k, outer_faces, 0, k)
        over_levels(k, outer_one, 0, k)
        fields = [(s1, f * cells) for f in mine]
        pack_columns(fields, ew_send2.at[g])
        columns_two.append(column_copies(1, g, ew_send2.at[g], ew_recv2.at[g]))
        for copy in columns_two[g]:
            copy.start()
        pack_rows(fields, ns_send2, g * per * k)
        mirror_rows(ns_send2, spans_two[g], False)
        rows_two.append(row_copies(1, g, ns_send2, ns_recv2, spans_two[g]))
        start_rows(rows_two[g])
        over_levels(k, inner_two, 0, 8)

    for g in groups:
        mine = range(g * per, (g + 1) * per)
        sides = y2.at[g]

        def forward(level, carry):
            c_side, c_south, c_north = (0.5 * tile(edge, level, i) for i in range(3))
            inverse, carried = tile(solve, level, 0), tile(solve, level, 2)
            now = []
            for i, f in enumerate(mine):
                south = ns_recv2[0, pl.ds(f * k + level, 1), :]
                north = ns_recv2[1, pl.ds(f * k + level, 1), :]
                added = c_side * side(sides, level, i) + (c_south * south + c_north * north)
                value = (tile(rhs, level, f) + added) * inverse + carried * carry[i]
                put(rhs, level, value, f)
                now.append(value)
            return tuple(now)

        def backward(level, carry):
            ratio = tile(solve, level, 1)
            now = []
            for i, f in enumerate(mine):
                value = tile(rhs, level, f) - ratio * carry[i]
                put(out, level, value, f)
                now.append(value)
            return tuple(now)

        for copy in columns_two[g]:
            copy.wait_recv()
        unpack_columns(ew_recv2.at[g], sides)
        rows_arrive(1, g, ns_send2, ns_recv2, spans_two[g])
        over_levels(k, forward, (zero,) * per, k)
        over_levels(k, backward, (zero,) * per, k, backward=True)

    for copy in columns_one:
        copy.wait_send()
    for g in groups:
        rows_one[g][0].wait_send()
        rows_two[g][0].wait_send()
        for copy in columns_two[g]:
            copy.wait_send()

    @pl.when(has_south)
    def _():
        for pair in rows_one + rows_two:
            pair[1].wait_send()


def on_device(n_lat, n_lon, tracer, east_vel, north_vel, wet_mask, bottom_level, vertical_mix):
    nt, k, rows, cols = tracer.shape
    cells = k * rows
    f32 = jnp.float32
    blocks = (nt + 2) * k * 2 // cols

    def vmem(*shape, dtype=f32):
        return pltpu.VMEM(shape, dtype)

    result = pl.pallas_call(
        functools.partial(kernel, nt, k, n_lat, n_lon),
        out_shape=pltpu.VMEM((nt * cells, cols), f32),
        in_specs=[pl.BlockSpec(memory_space=pltpu.HBM)] * 6,
        out_specs=pl.BlockSpec(memory_space=pltpu.VMEM),
        scratch_shapes=[
            vmem(nt * cells, cols),
            vmem(cells, cols),
            vmem(cells, cols),
            vmem(cells, cols, dtype=jnp.int32),
            vmem(rows, cols, dtype=jnp.int32),
            vmem(cells, cols),
            vmem(cells, cols),
            vmem(nt * cells, cols),
            vmem(nt * cells, cols),
            vmem(blocks, rows, cols),
            vmem(GROUPS, 1, rows, cols),
            vmem(5 * cells, cols),
            vmem(4 * cells, cols),
            vmem(3 * cells, cols),
            vmem(2, (nt + 2) * k, cols),
            vmem(2, (nt + 2) * k, cols),
            vmem(blocks, rows, cols),
            vmem(2, blocks, rows, cols),
            vmem(2, nt * k, cols),
            vmem(2, nt * k, cols),
            vmem(GROUPS, 1, rows, cols),
            vmem(GROUPS, 2, 1, rows, cols),
            pltpu.SemaphoreType.DMA((5 + GROUPS,)),
            pltpu.SemaphoreType.DMA((2, GROUPS, 4)),
            pltpu.SemaphoreType.DMA((2, GROUPS, 4)),
        ],
        compiler_params=pltpu.CompilerParams(
            collective_id=0, has_side_effects=True, vmem_limit_bytes=62 * 1024 * 1024
        ),
    )(
        tracer.reshape(nt * cells, cols),
        east_vel.reshape(cells, cols),
        north_vel.reshape(cells, cols),
        wet_mask.reshape(cells, cols),
        bottom_level,
        vertical_mix.reshape(cells, cols),
    )
    return result.reshape(tracer.shape)


def solution(mesh):
    in_specs = (
        P(None, None, "lat", "lon"),
        P(None, "lat", "lon"),
        P(None, "lat", "lon"),
        P(None, "lat", "lon"),
        P("lat", "lon"),
        P(None, "lat", "lon"),
    )
    out_specs = P(None, None, "lat", "lon")
    return jax.shard_map(
        functools.partial(on_device, mesh.shape["lat"], mesh.shape["lon"]),
        mesh=mesh, in_specs=in_specs, out_specs=out_specs, check_vma=False,
    )
```
